512 devices in a mesh: batch: 16 (over z), proto: 32 (over y, x, core).
Axes of the slice: x: 4, y: 4, z: 16, core: 2. Of those that a mesh axis runs over, the one named last changes fastest.
Arguments:
- teacher_feats: bfloat16 [4096, 256], P('batch'), may hold values from -2 to 2
- student_feats: bfloat16 [4096, 256], P('batch'), may hold values from -2 to 2
- teacher_weight: bfloat16 [256, 131072], P(None, 'proto'), may hold values from -2 to 2
- student_weight: bfloat16 [256, 131072], P(None, 'proto'), may hold values from -2 to 2
Outputs:
- weight_grad: bfloat16 [256, 131072], P('batch', 'proto')
- feature_grad: bfloat16 [4096, 256], P('batch')
The draws below stay inside these ranges and needn't reach their ends.
All inputs are finite; a program needn't handle non-finite values.
Results may differ from the reference program's by a relative error of at most 0.025.
Values may be sent and summed in bfloat16 or wider, within the bound.
A program may use at most 64 MiB of HBM per device.

```python
import math
import jax
import jax.numpy as jnp
from jax import lax

D = 256
B_DEV = 256
ITERS = 3
CLUSTERS = 64
PROTOS = 131072
CROPS = 4096


def cluster_parts(key):
    centres = jax.random.normal(jax.random.fold_in(key, 101), (CLUSTERS, D), jnp.float32)
    crop_ids = jnp.sort(jax.random.randint(jax.random.fold_in(key, 102), (CROPS,), 0, CLUSTERS))
    first_ids = jax.random.randint(jax.random.fold_in(key, 103), (PROTOS,), 0, CLUSTERS)
    second_ids = jax.random.randint(jax.random.fold_in(key, 104), (PROTOS,), 0, CLUSTERS)
    proto_ids = jnp.sort(jnp.minimum(first_ids, second_ids))
    crop_shared = jax.random.normal(jax.random.fold_in(key, 105), (CROPS, D), jnp.float32)
    proto_shared = jax.random.normal(jax.random.fold_in(key, 106), (D, PROTOS), jnp.float32)
    return (centres, crop_ids, proto_ids, crop_shared, proto_shared)


def draw_teacher_feats(key, part):
    centres, crop_ids, proto_ids, crop_shared, proto_shared = cluster_parts(key)
    key = jax.random.fold_in(key, 1)
    strength = 0.65
    noise = jax.random.normal(key, (CROPS, D), jnp.float32)
    values = (strength * centres[crop_ids] + 0.7 * crop_shared + 0.7 * noise) / 16.0
    return jnp.clip(values, -2.0, 2.0).astype(jnp.bfloat16)


def draw_student_feats(key, part):
    centres, crop_ids, proto_ids, crop_shared, proto_shared = cluster_parts(key)
    key = jax.random.fold_in(key, 2)
    strength = 0.65
    noise = jax.random.normal(key, (CROPS, D), jnp.float32)
    values = (strength * centres[crop_ids] + 0.7 * crop_shared + 0.7 * noise) / 16.0
    return jnp.clip(values, -2.0, 2.0).astype(jnp.bfloat16)


def draw_teacher_weight(key, part):
    centres, crop_ids, proto_ids, crop_shared, proto_shared = cluster_parts(key)
    key = jax.random.fold_in(key, 3)
    strength = 0.65
    noise = jax.random.normal(key, (D, PROTOS), jnp.float32)
    values = (strength * centres[proto_ids].T + 0.7 * proto_shared + 0.7 * noise) / 16.0
    return jnp.clip(values, -2.0, 2.0).astype(jnp.bfloat16)


def draw_student_weight(key, part):
    centres, crop_ids, proto_ids, crop_shared, proto_shared = cluster_parts(key)
    key = jax.random.fold_in(key, 4)
    strength = 0.65
    noise = jax.random.normal(key, (D, PROTOS), jnp.float32)
    values = (strength * centres[proto_ids].T + 0.7 * proto_shared + 0.7 * noise) / 16.0
    return jnp.clip(values, -2.0, 2.0).astype(jnp.bfloat16)


def setup_inputs(seed: int = 0) -> dict:
    seeds = jax.random.split(jax.random.key(seed), 5)
    teacher_feats = draw_teacher_feats(jax.random.fold_in(seeds[4], 71), 0)
    student_feats = draw_student_feats(jax.random.fold_in(seeds[4], 71), 0)
    teacher_weight = draw_teacher_weight(jax.random.fold_in(seeds[4], 71), 0)
    student_weight = draw_student_weight(jax.random.fold_in(seeds[4], 71), 0)
    return dict(teacher_feats=teacher_feats, student_feats=student_feats, teacher_weight=teacher_weight, student_weight=student_weight)


teacher_temp = 0.07
student_temp = 0.1
epsilon = 1e-06

def unit_rows(raw):
    values = raw.astype(jnp.float32)
    length = jnp.sqrt(lax.optimization_barrier(jnp.sum(values * values, axis=1, keepdims=True)) + epsilon)
    return (values / length, length)

def unit_columns(raw):
    values = raw.astype(jnp.float32)
    length = jnp.sqrt(lax.optimization_barrier(jnp.sum(values * values, axis=0, keepdims=True)) + epsilon)
    return (values / length).astype(jnp.bfloat16)

def reference(teacher_feats, student_feats, teacher_weight, student_weight):
    teacher_unit, _ = unit_rows(teacher_feats)
    teacher_half = teacher_unit.astype(jnp.bfloat16)
    student_unit, student_len = unit_rows(student_feats)
    student_half = student_unit.astype(jnp.bfloat16)
    teacher_cols = unit_columns(teacher_weight)
    student_cols = unit_columns(student_weight)
    groups = CROPS // B_DEV
    teacher_blocks = teacher_half.reshape(groups, B_DEV, D)

    def teacher_exp(block):
        return jnp.exp(jnp.dot(block, teacher_cols, preferred_element_type=jnp.float32) / teacher_temp)
    crop_scale = jnp.ones((groups, B_DEV), jnp.float32)
    proto_scale = jnp.ones((PROTOS,), jnp.float32)
    for sweep_index in range(ITERS):

        def add_rows(total, item):
            block, scale = item
            return (total + lax.optimization_barrier(jnp.sum(teacher_exp(block) * scale[:, None], axis=0)), None)
        sums, _ = lax.scan(add_rows, jnp.zeros((PROTOS,), jnp.float32), (teacher_blocks, crop_scale))
        proto_scale = 1.0 / sums

        def crop_total(block):
            return lax.optimization_barrier(jnp.sum(teacher_exp(block) * proto_scale[None, :], axis=1))
        crop_scale = 1.0 / lax.map(crop_total, teacher_blocks)
    weight_factor = math.sqrt(D / CROPS)
    feature_factor = math.sqrt(D / PROTOS)

    def finish(carry, item):
        tblock, sblock, sfull, slength, scale = item
        targets = teacher_exp(tblock) * proto_scale[None, :] * scale[:, None]
        logits = jnp.dot(sblock, student_cols, preferred_element_type=jnp.float32) / student_temp
        log_total = jnp.log(lax.optimization_barrier(jnp.sum(jnp.exp(logits), axis=1, keepdims=True)))
        student_prob = jnp.exp(logits - log_total)
        grad_logits = (PROTOS * (student_prob - targets)).astype(jnp.bfloat16)
        partial_value = lax.dot_general(sblock, grad_logits, (((0,), (0,)), ((), ())), preferred_element_type=jnp.float32) * weight_factor
        partial_value = lax.optimization_barrier(partial_value.astype(jnp.bfloat16)).astype(jnp.float32)
        unit_grad = lax.dot_general(grad_logits, student_cols, (((1,), (1,)), ((), ())), preferred_element_type=jnp.float32) * feature_factor
        along = lax.optimization_barrier(jnp.sum(sfull * unit_grad, axis=1, keepdims=True))
        rows_grad = ((unit_grad - sfull * along) / slength).astype(jnp.bfloat16)
        return (carry + partial_value, rows_grad)
    start = jnp.zeros((D, PROTOS), jnp.float32)
    items = (teacher_blocks, student_half.reshape(groups, B_DEV, D), student_unit.reshape(groups, B_DEV, D), student_len.reshape(groups, B_DEV, 1), crop_scale)
    weight_total, rows_all = lax.scan(finish, start, items)
    return (weight_total.astype(jnp.bfloat16), rows_all.reshape(CROPS, D))
```

```python
import functools
import math

import jax
import jax.numpy as jnp
from jax import lax
from jax.experimental import pallas as pl
from jax.experimental.pallas import tpu as pltpu
from jax.sharding import PartitionSpec as P

ITERS = 3
TEACHER_TEMP = 0.07
STUDENT_TEMP = 0.1
EPSILON = 1e-06
MESH = pl.DeviceIdType.MESH

NZ = 16
NJ = 32
D = 256
B = 256
C = 4096
PROTOS = C * NJ
CROPS = B * NZ
LANES = 128
TILES = C // LANES
WIDE = 256
WTILES = C // WIDE
ROWS = D // NZ
SUBS = 4
SUB = C // SUBS
STEPS = NZ // 2
FROWS = B // NJ


def kernel(
    tf_ref, sf_ref, tw_ref, sw_ref, wout_ref, fout_ref,
    e_ref, s_ref, ws_ref, wpart_ref, ring_ref,
    zt_ref, zs_ref, zst_ref, zfull_ref, zlen_ref,
    pr_ref, pf_ref, psend_ref, pbuf_ref, u_ref, crep_ref, srep_ref,
    csend_ref, cbuf_ref, ssend_ref, sbuf_ref,
    fsend_ref, fbuf_ref, gsend_ref, gbuf_ref,
    psend_sem, precv_sem, csend_sem, crecv_sem, ssend_sem, srecv_sem,
    fsend_sem, frecv_sem, gsend_sem, grecv_sem, wsend_sem, wrecv_sem,
):
    z = lax.axis_index("batch")
    j = lax.axis_index("proto")

    def zpeer(k):
        return (lax.rem(z + k, NZ), j)

    def jpeer(k):
        return (z, lax.rem(j + k, NJ))

    barrier = pltpu.get_barrier_semaphore()
    for k in range(1, NJ):
        pl.semaphore_signal(barrier, 1, device_id=jpeer(k), device_id_type=MESH)
    for k in range(1, NZ):
        pl.semaphore_signal(barrier, 1, device_id=zpeer(k), device_id_type=MESH)

    tf = tf_ref[...].astype(jnp.float32)
    tlen = jnp.sqrt(jnp.sum(tf * tf, axis=1, keepdims=True) + EPSILON)
    zt_ref[...] = (tf / tlen).astype(jnp.bfloat16)

    def columns(t):
        return pl.ds(pl.multiple_of(t * WIDE, WIDE), WIDE)

    def unit_columns(raw):
        values = raw.astype(jnp.float32)
        length = jnp.sqrt(jnp.sum(values * values, axis=0, keepdims=True) + EPSILON)
        return (values / length).astype(jnp.bfloat16)

    def teacher_tile(t, carry):
        wt = unit_columns(tw_ref[:, columns(t)])
        dots = jnp.dot(zt_ref[...], wt, preferred_element_type=jnp.float32)
        e = jnp.exp(dots * (1.0 / TEACHER_TEMP))
        e_ref[2 * t] = e[:, :LANES]
        e_ref[2 * t + 1] = e[:, LANES:]
        pr_ref[t] = jnp.sum(e, axis=0, keepdims=True)
        return carry

    lax.fori_loop(0, WTILES, teacher_tile, 0)

    def send_protos(it):
        pf_ref[...] = jnp.concatenate([pr_ref[t] for t in range(WTILES)], axis=0)
        psend_ref[it] = pf_ref[...].astype(jnp.bfloat16)
        for k in range(1, NZ):
            pltpu.make_async_remote_copy(
                src_ref=psend_ref.at[it],
                dst_ref=pbuf_ref.at[it, k - 1],
                send_sem=psend_sem.at[it],
                recv_sem=precv_sem.at[it],
                device_id=zpeer(k),
                device_id_type=MESH,
            ).start()

    def receive_protos(it):
        whole = pbuf_ref.at[it]
        pltpu.make_async_copy(whole, whole, precv_sem.at[it]).wait()
        total = pf_ref[...]
        for k in range(NZ - 1):
            total = total + pbuf_ref[it, k].astype(jnp.float32)
        scale = 1.0 / total
        for t in range(WTILES):
            u_ref[t] = scale[t:t + 1]

    pl.semaphore_wait(barrier, NJ + NZ - 2)
    send_protos(0)

    sf = sf_ref[...].astype(jnp.float32)
    slen = jnp.sqrt(jnp.sum(sf * sf, axis=1, keepdims=True) + EPSILON)
    sfull = sf / slen
    zfull_ref[...] = sfull
    zlen_ref[...] = jnp.broadcast_to(slen, (B, LANES))
    zs_ref[...] = sfull.astype(jnp.bfloat16)
    zst_ref[...] = jnp.transpose(sfull).astype(jnp.bfloat16)

    def student_tile(t, acc):
        ws = unit_columns(sw_ref[:, columns(t)])
        ws_ref[:, columns(t)] = ws
        dots = jnp.dot(zs_ref[...], ws, preferred_element_type=jnp.float32)
        s = jnp.exp(dots * (1.0 / STUDENT_TEMP))
        s_ref[2 * t] = s[:, :LANES]
        s_ref[2 * t + 1] = s[:, LANES:]
        return acc + s[:, :LANES] + s[:, LANES:]

    sacc = lax.fori_loop(0, WTILES, student_tile, jnp.zeros((B, LANES), jnp.float32))
    ssend_ref[...] = jnp.sum(jnp.transpose(sacc), axis=0, keepdims=True)
    for k in range(1, NJ):
        pltpu.make_async_remote_copy(
            src_ref=ssend_ref,
            dst_ref=sbuf_ref.at[k - 1],
            send_sem=ssend_sem,
            recv_sem=srecv_sem,
            device_id=jpeer(k),
            device_id_type=MESH,
        ).start()

    for it in range(ITERS):
        if it > 0:
            def proto_tile(t, carry):
                c = crep_ref[...]
                for h in range(2):
                    pr_ref[t, :, h * LANES:(h + 1) * LANES] = jnp.sum(
                        e_ref[2 * t + h] * c, axis=0, keepdims=True
                    )
                return carry

            lax.fori_loop(0, WTILES, proto_tile, 0)
            send_protos(it)
        receive_protos(it)
        last = it == ITERS - 1

        def crop_tile(t, acc):
            for h in range(2):
                scaled = e_ref[2 * t + h] * u_ref[t, :, h * LANES:(h + 1) * LANES]
                if last:
                    e_ref[2 * t + h] = scaled
                acc = acc + scaled
            return acc

        acc = lax.fori_loop(0, WTILES, crop_tile, jnp.zeros((B, LANES), jnp.float32))
        row = jnp.sum(jnp.transpose(acc), axis=0, keepdims=True)
        csend_ref[it] = row
        for k in range(1, NJ):
            pltpu.make_async_remote_copy(
                src_ref=csend_ref.at[it],
                dst_ref=cbuf_ref.at[it, k - 1],
                send_sem=csend_sem.at[it],
                recv_sem=crecv_sem.at[it],
                device_id=jpeer(k),
                device_id_type=MESH,
            ).start()
        got = cbuf_ref.at[it]
        pltpu.make_async_copy(got, got, crecv_sem.at[it]).wait()
        for k in range(NJ - 1):
            row = row + cbuf_ref[it, k]
        crop_scale = 1.0 / row
        if last:
            crop_scale = crop_scale * float(PROTOS)
        crep_ref[...] = jnp.transpose(jnp.broadcast_to(crop_scale, (LANES, B)))

    pltpu.make_async_copy(sbuf_ref, sbuf_ref, srecv_sem).wait()
    row = ssend_ref[...]
    for k in range(NJ - 1):
        row = row + sbuf_ref[k]
    inverse = float(PROTOS) / row
    srep_ref[...] = jnp.transpose(jnp.broadcast_to(inverse, (LANES, B)))
    weight_factor = math.sqrt(D / CROPS)
    feature_factor = math.sqrt(D / PROTOS)

    def grad_tile(t, acc):
        c = crep_ref[...]
        halves = [s_ref[2 * t + h] * srep_ref[...] - e_ref[2 * t + h] * c for h in range(2)]
        grad = jnp.concatenate([half.astype(jnp.bfloat16) for half in halves], axis=1)
        term = jnp.dot(zst_ref[...], grad, preferred_element_type=jnp.float32)
        wpart_ref[:, columns(t)] = (term * weight_factor).astype(jnp.bfloat16)
        return acc + lax.dot_general(
            grad, ws_ref[:, columns(t)], (((1,), (1,)), ((), ())), preferred_element_type=jnp.float32
        )

    feature = lax.fori_loop(0, WTILES, grad_tile, jnp.zeros((B, D), jnp.float32))

    def chunk(distance, sub):
        target = lax.rem(z + distance, NZ)
        return wpart_ref.at[pl.ds(pl.multiple_of(target * ROWS, ROWS), ROWS), pl.ds(sub * SUB, SUB)]

    def subs_of(way, step):
        half = SUBS // 2
        if step > 0:
            return tuple(range(SUBS))
        return tuple(range(half)) if way == 0 else tuple(range(half, SUBS))

    def ring_copy(way, step, sub):
        distance = STEPS - step if way == 0 else NZ - (STEPS - step)
        return pltpu.make_async_remote_copy(
            src_ref=chunk(distance, sub),
            dst_ref=ring_ref.at[way, step, :, pl.ds(sub * SUB, SUB)],
            send_sem=wsend_sem.at[way, step, sub],
            recv_sem=wrecv_sem.at[way, step, sub],
            device_id=zpeer(1 if way == 0 else NZ - 1),
            device_id_type=MESH,
        )

    def ring_step(step):
        for sub in range(SUBS):
            for way in range(2):
                if sub not in subs_of(way, step):
                    continue
                copy = ring_copy(way, step, sub)
                if step > 0 and sub in subs_of(way, step - 1):
                    ring_copy(way, step - 1, sub).wait_recv()
                    distance = STEPS - step if way == 0 else NZ - (STEPS - step)
                    own = chunk(distance, sub)
                    arrived = ring_ref[way, step - 1, :, sub * SUB:(sub + 1) * SUB]
                    own[...] = (own[...].astype(jnp.float32) + arrived.astype(jnp.float32)).astype(jnp.bfloat16)
                copy.start()

    ring_step(0)

    feature = feature * feature_factor
    for i in range(NJ):
        rows = feature[i * FROWS:(i + 1) * FROWS]
        fsend_ref[i] = jnp.concatenate([rows[:, :LANES], rows[:, LANES:]], axis=0).astype(jnp.bfloat16)
    for k in range(1, NJ):
        pltpu.make_async_remote_copy(
            src_ref=fsend_ref.at[lax.rem(j + k, NJ)],
            dst_ref=fbuf_ref.at[k - 1],
            send_sem=fsend_sem,
            recv_sem=frecv_sem,
            device_id=jpeer(k),
            device_id_type=MESH,
        ).start()

    ring_step(1)
    ring_step(2)

    whole = fbuf_ref
    pltpu.make_async_copy(whole, whole, frecv_sem).wait()
    total = fsend_ref[j].astype(jnp.float32)
    for k in range(NJ - 1):
        total = total + fbuf_ref[k].astype(jnp.float32)
    unit_grad = jnp.concatenate([total[:FROWS], total[FROWS:]], axis=1)
    mine = pl.ds(pl.multiple_of(j * FROWS, FROWS), FROWS)
    unit = zfull_ref[mine, :]
    along = jnp.sum(unit * unit_grad, axis=1, keepdims=True)
    length = zlen_ref[mine, :]
    rows = unit_grad - unit * along
    gsend_ref[...] = jnp.concatenate([rows[:, :LANES] / length, rows[:, LANES:] / length], axis=0).astype(jnp.bfloat16)
    for k in range(1, NJ):
        pltpu.make_async_remote_copy(
            src_ref=gsend_ref,
            dst_ref=gbuf_ref.at[j],
            send_sem=gsend_sem,
            recv_sem=grecv_sem,
            device_id=jpeer(k),
            device_id_type=MESH,
        ).start()
    gbuf_ref[j] = gsend_ref[...]

    for step in range(3, STEPS):
        ring_step(step)

    got = gbuf_ref.at[pl.ds(0, NJ - 1)]
    pltpu.make_async_copy(got, got, grecv_sem).wait()
    for i in range(NJ // 2):
        one = gbuf_ref[2 * i].astype(jnp.float32)
        two = gbuf_ref[2 * i + 1].astype(jnp.float32)
        left = jnp.concatenate([one[:FROWS], two[:FROWS]], axis=0)
        right = jnp.concatenate([one[FROWS:], two[FROWS:]], axis=0)
        fout_ref[2 * FROWS * i:2 * FROWS * (i + 1), :] = jnp.concatenate([left, right], axis=1).astype(jnp.bfloat16)

    for sub in range(SUBS):
        at = pl.ds(sub * SUB, SUB)
        total = chunk(0, sub)[...].astype(jnp.float32)
        for way in range(2):
            ring_copy(way, STEPS - 1, sub).wait_recv()
            total = total + ring_ref[way, STEPS - 1, :, at].astype(jnp.float32)
        wout_ref[:, at] = total.astype(jnp.bfloat16)

    for it in range(ITERS):
        whole = pbuf_ref.at[it]
        pltpu.make_async_copy(whole, whole, psend_sem.at[it]).wait()
        got = cbuf_ref.at[it]
        pltpu.make_async_copy(got, got, csend_sem.at[it]).wait()
    pltpu.make_async_copy(sbuf_ref, sbuf_ref, ssend_sem).wait()
    pltpu.make_async_copy(fbuf_ref, fbuf_ref, fsend_sem).wait()
    pltpu.make_async_copy(fbuf_ref, fbuf_ref, gsend_sem).wait()
    for step in range(STEPS):
        for way in range(2):
            for sub in subs_of(way, step):
                ring_copy(way, step, sub).wait_send()


def shards(teacher_feats, student_feats, teacher_weight, student_weight):
    f32, bf16 = jnp.float32, jnp.bfloat16
    vmem, dma = pltpu.VMEM, pltpu.SemaphoreType.DMA
    scratch = [
        vmem((TILES, B, LANES), f32),
        vmem((TILES, B, LANES), f32),
        vmem((D, C), bf16),
        vmem((D, C), bf16),
        vmem((2, STEPS, ROWS, C), bf16),
        vmem((B, D), bf16),
        vmem((B, D), bf16),
        vmem((D, B), bf16),
        vmem((B, D), f32),
        vmem((B, LANES), f32),
        vmem((WTILES, 1, WIDE), f32),
        vmem((WTILES, WIDE), f32),
        vmem((ITERS, WTILES, WIDE), bf16),
        vmem((ITERS, NZ - 1, WTILES, WIDE), bf16),
        vmem((WTILES, 1, WIDE), f32),
        vmem((B, LANES), f32),
        vmem((B, LANES), f32),
        vmem((ITERS, 1, B), f32),
        vmem((ITERS, NJ - 1, 1, B), f32),
        vmem((1, B), f32),
        vmem((NJ - 1, 1, B), f32),
        vmem((NJ, 2 * FROWS, LANES), bf16),
        vmem((NJ - 1, 2 * FROWS, LANES), bf16),
        vmem((2 * FROWS, LANES), bf16),
        vmem((NJ, 2 * FROWS, LANES), bf16),
        dma((ITERS,)), dma((ITERS,)), dma((ITERS,)), dma((ITERS,)), dma, dma,
        dma, dma, dma, dma, dma((2, STEPS, SUBS)), dma((2, STEPS, SUBS)),
    ]
    return pl.pallas_call(
        kernel,
        out_shape=(jax.ShapeDtypeStruct((ROWS, C), bf16), jax.ShapeDtypeStruct((B, D), bf16)),
        in_specs=[pl.BlockSpec(memory_space=pltpu.VMEM)] * 4,
        out_specs=(pl.BlockSpec(memory_space=pltpu.VMEM), pl.BlockSpec(memory_space=pltpu.VMEM)),
        scratch_shapes=scratch,
        compiler_params=pltpu.CompilerParams(
            collective_id=0, has_side_effects=True, vmem_limit_bytes=48 << 20
        ),
        cost_estimate=pl.CostEstimate(
            flops=8 * B * C * D, bytes_accessed=4 * D * C + 6 * B * D, transcendentals=2 * B * C
        ),
    )(teacher_feats, student_feats, teacher_weight, student_weight)


def solution(mesh):
    return jax.shard_map(
        shards,
        mesh=mesh,
        in_specs=(P("batch", None), P("batch", None), P(None, "proto"), P(None, "proto")),
        out_specs=(P("batch", "proto"), P("batch", None)),
        check_vma=False,
    )
```

```python
import functools
import math

import jax
import jax.numpy as jnp
from jax import lax
from jax.experimental import pallas as pl
from jax.experimental.pallas import tpu as pltpu
from jax.sharding import PartitionSpec as P

ITERS = 3
TEACHER_TEMP = 0.07
STUDENT_TEMP = 0.1
EPSILON = 1e-06
MESH = pl.DeviceIdType.MESH

NZ = 16
NJ = 32
D = 256
B = 256
C = 4096
PROTOS = C * NJ
CROPS = B * NZ
LANES = 128
TILES = C // LANES
WIDE = 256
WTILES = C // WIDE
PARTS = 4
PART = C // PARTS
ROWS = D // NZ
SUBS = 4
SUB = C // SUBS
STEPS = NZ // 2
FROWS = B // NJ
Z_ORDER = sorted(range(1, NZ), key=lambda k: -min(k, NZ - k))


def kernel(
    tf_hbm, sf_hbm, tw_hbm, sw_hbm, wout_ref, fout_ref,
    tf_ref, sf_ref, tw_ref, sw_ref,
    e_ref, s_ref, ws_ref, grad_ref, wpart_ref, ring_ref,
    zt_ref, zs_ref, zst_ref, zfull_ref, zlen_ref,
    pr_ref, pf_ref, psend_ref, pbuf_ref, u_ref, crep_ref, srep_ref,
    csend_ref, cbuf_ref, ssend_ref, sbuf_ref,
    fsend_ref, fbuf_ref, gsend_ref, gbuf_ref,
    psend_sem, precv_sem, csend_sem, crecv_sem, ssend_sem, srecv_sem,
    fsend_sem, frecv_sem, gsend_sem, grecv_sem, wsend_sem, wrecv_sem, load_sem, tload_sem,
):
    z = lax.axis_index("batch")
    j = lax.axis_index("proto")

    def zpeer(k):
        return (lax.rem(z + k, NZ), j)

    def jpeer(k):
        return (z, lax.rem(j + k, NJ))

    barrier = pltpu.get_barrier_semaphore()
    for k in range(1, NJ):
        pl.semaphore_signal(barrier, 1, device_id=jpeer(k), device_id_type=MESH)
    for k in Z_ORDER:
        pl.semaphore_signal(barrier, 1, device_id=zpeer(k), device_id_type=MESH)

    load_tf = pltpu.make_async_copy(tf_hbm, tf_ref, load_sem.at[0])
    load_sf = pltpu.make_async_copy(sf_hbm, sf_ref, load_sem.at[1])
    load_sw = pltpu.make_async_copy(sw_hbm, sw_ref, load_sem.at[2])

    def load_tw(part):
        at = pl.ds(pl.multiple_of(part * PART, PART), PART)
        return pltpu.make_async_copy(tw_hbm.at[:, at], tw_ref.at[:, at], tload_sem.at[part])

    load_tf.start()
    for part in range(PARTS):
        load_tw(part).start()
    load_sf.start()
    load_sw.start()
    load_tf.wait()

    tf = tf_ref[...].astype(jnp.float32)
    zt_ref[...] = (tf * lax.rsqrt(jnp.sum(tf * tf, axis=1, keepdims=True) + EPSILON)).astype(jnp.bfloat16)

    def columns(t):
        return pl.ds(pl.multiple_of(t * WIDE, WIDE), WIDE)

    def inverse_lengths(values):
        return lax.rsqrt(jnp.sum(values * values, axis=0, keepdims=True) + EPSILON)

    def teacher_tile(t, carry):
        raw = tw_ref[:, columns(t)]
        scale = inverse_lengths(raw.astype(jnp.float32)) * (1.0 / TEACHER_TEMP)
        dots = jnp.dot(zt_ref[...], raw, preferred_element_type=jnp.float32)
        e = jnp.exp(dots * scale)
        e_ref[2 * t] = e[:, :LANES]
        e_ref[2 * t + 1] = e[:, LANES:]
        pr_ref[t] = jnp.sum(e, axis=0, keepdims=True)
        return carry

    for part in range(PARTS):
        load_tw(part).wait()
        lax.fori_loop(part * (WTILES // PARTS), (part + 1) * (WTILES // PARTS), teacher_tile, 0, unroll=True)

    def send_protos(it):
        pf_ref[...] = jnp.concatenate([pr_ref[t] for t in range(WTILES)], axis=0)
        psend_ref[it] = pf_ref[...].astype(jnp.bfloat16)
        for k in Z_ORDER:
            pltpu.make_async_remote_copy(
                src_ref=psend_ref.at[it],
                dst_ref=pbuf_ref.at[it, k - 1],
                send_sem=psend_sem.at[it],
                recv_sem=precv_sem.at[it],
                device_id=zpeer(k),
                device_id_type=MESH,
            ).start()

    def receive_protos(it):
        whole = pbuf_ref.at[it]
        pltpu.make_async_copy(whole, whole, precv_sem.at[it]).wait()
        total = pf_ref[...]
        for k in range(NZ - 1):
            total = total + pbuf_ref[it, k].astype(jnp.float32)
        scale = 1.0 / total
        for t in range(WTILES):
            u_ref[t] = scale[t:t + 1]

    pl.semaphore_wait(barrier, NJ + NZ - 2)
    send_protos(0)

    load_sf.wait()
    load_sw.wait()
    sf = sf_ref[...].astype(jnp.float32)
    slen = jnp.sqrt(jnp.sum(sf * sf, axis=1, keepdims=True) + EPSILON)
    sfull = sf / slen
    zfull_ref[...] = sfull
    zlen_ref[...] = jnp.broadcast_to(slen, (B, LANES))
    zs_ref[...] = sfull.astype(jnp.bfloat16)
    zst_ref[...] = jnp.transpose(sfull).astype(jnp.bfloat16)

    def student_tile(t, acc):
        values = sw_ref[:, columns(t)].astype(jnp.float32)
        ws = (values * inverse_lengths(values)).astype(jnp.bfloat16)
        ws_ref[:, columns(t)] = ws
        dots = jnp.dot(zs_ref[...], ws, preferred_element_type=jnp.float32)
        s = jnp.exp(dots * (1.0 / STUDENT_TEMP))
        s_ref[2 * t] = s[:, :LANES]
        s_ref[2 * t + 1] = s[:, LANES:]
        return acc + s[:, :LANES] + s[:, LANES:]

    sacc = lax.fori_loop(0, WTILES, student_tile, jnp.zeros((B, LANES), jnp.float32), unroll=2)
    ssend_ref[...] = jnp.sum(jnp.transpose(sacc), axis=0, keepdims=True)
    for k in range(1, NJ):
        pltpu.make_async_remote_copy(
            src_ref=ssend_ref,
            dst_ref=sbuf_ref.at[k - 1],
            send_sem=ssend_sem,
            recv_sem=srecv_sem,
            device_id=jpeer(k),
            device_id_type=MESH,
        ).start()

    for it in range(ITERS):
        if it > 0:
            def proto_tiles(g, carry):
                totals = [None] * 4
                for r in range(0, B, 8):
                    c = crep_ref[r:r + 8]
                    for i in range(4):
                        term = e_ref[4 * g + i, r:r + 8] * c
                        totals[i] = term if r == 0 else totals[i] + term
                for i in range(4):
                    pr_ref[2 * g + i // 2, :, (i % 2) * LANES:(i % 2 + 1) * LANES] = jnp.sum(
                        totals[i], axis=0, keepdims=True
                    )
                return carry

            lax.fori_loop(0, TILES // 4, proto_tiles, 0, unroll=2)
            send_protos(it)
        receive_protos(it)
        last = it == ITERS - 1

        def crop_tile(t, acc):
            for h in range(2):
                scaled = e_ref[2 * t + h] * u_ref[t, :, h * LANES:(h + 1) * LANES]
                if last:
                    e_ref[2 * t + h] = scaled
                acc = acc + scaled
            return acc

        acc = lax.fori_loop(0, WTILES, crop_tile, jnp.zeros((B, LANES), jnp.float32), unroll=4)
        row = jnp.sum(jnp.transpose(acc), axis=0, keepdims=True)
        csend_ref[it] = row
        for k in range(1, NJ):
            pltpu.make_async_remote_copy(
                src_ref=csend_ref.at[it],
                dst_ref=cbuf_ref.at[it, k - 1],
                send_sem=csend_sem.at[it],
                recv_sem=crecv_sem.at[it],
                device_id=jpeer(k),
                device_id_type=MESH,
            ).start()
        got = cbuf_ref.at[it]
        pltpu.make_async_copy(got, got, crecv_sem.at[it]).wait()
        for k in range(NJ - 1):
            row = row + cbuf_ref[it, k]
        crop_scale = 1.0 / row
        if last:
            crop_scale = crop_scale * float(PROTOS)
        crep_ref[...] = jnp.transpose(jnp.broadcast_to(crop_scale, (LANES, B)))

    pltpu.make_async_copy(sbuf_ref, sbuf_ref, srecv_sem).wait()
    row = ssend_ref[...]
    for k in range(NJ - 1):
        row = row + sbuf_ref[k]
    inverse = float(PROTOS) / row
    srep_ref[...] = jnp.transpose(jnp.broadcast_to(inverse, (LANES, B)))
    weight_factor = math.sqrt(D / CROPS)
    feature_factor = math.sqrt(D / PROTOS)

    def grad_tile(t, carry):
        c = crep_ref[...]
        halves = [s_ref[2 * t + h] * srep_ref[...] - e_ref[2 * t + h] * c for h in range(2)]
        grad = jnp.concatenate([half.astype(jnp.bfloat16) for half in halves], axis=1)
        term = jnp.dot(zst_ref[...], grad, preferred_element_type=jnp.float32)
        wpart_ref[:, columns(t)] = (term * weight_factor).astype(jnp.bfloat16)
        grad_ref[:, columns(t)] = grad
        return carry

    lax.fori_loop(0, WTILES, grad_tile, 0, unroll=4)

    def chunk(distance, sub):
        target = lax.rem(z + distance, NZ)
        return wpart_ref.at[pl.ds(pl.multiple_of(target * ROWS, ROWS), ROWS), pl.ds(sub * SUB, SUB)]

    def subs_of(way, step):
        half = SUBS // 2
        if step > 0:
            return tuple(range(SUBS))
        return tuple(range(half)) if way == 0 else tuple(range(half, SUBS))

    def ring_copy(way, step, sub):
        distance = STEPS - step if way == 0 else NZ - (STEPS - step)
        return pltpu.make_async_remote_copy(
            src_ref=chunk(distance, sub),
            dst_ref=ring_ref.at[way, step, :, pl.ds(sub * SUB, SUB)],
            send_sem=wsend_sem.at[way, step, sub],
            recv_sem=wrecv_sem.at[way, step, sub],
            device_id=zpeer(1 if way == 0 else NZ - 1),
            device_id_type=MESH,
        )

    def ring_step(step):
        for sub in range(SUBS):
            for way in range(2):
                if sub not in subs_of(way, step):
                    continue
                copy = ring_copy(way, step, sub)
                if step > 0 and sub in subs_of(way, step - 1):
                    ring_copy(way, step - 1, sub).wait_recv()
                    distance = STEPS - step if way == 0 else NZ - (STEPS - step)
                    own = chunk(distance, sub)
                    arrived = ring_ref[way, step - 1, :, sub * SUB:(sub + 1) * SUB]
                    own[...] = (own[...].astype(jnp.float32) + arrived.astype(jnp.float32)).astype(jnp.bfloat16)
                copy.start()

    ring_step(0)

    feature = lax.dot_general(
        grad_ref[...], ws_ref[...], (((1,), (1,)), ((), ())), preferred_element_type=jnp.float32
    ) * feature_factor
    for i in range(NJ):
        rows = feature[i * FROWS:(i + 1) * FROWS]
        fsend_ref[i] = jnp.concatenate([rows[:, :LANES], rows[:, LANES:]], axis=0).astype(jnp.bfloat16)
    for k in range(1, NJ):
        pltpu.make_async_remote_copy(
            src_ref=fsend_ref.at[lax.rem(j + k, NJ)],
            dst_ref=fbuf_ref.at[k - 1],
            send_sem=fsend_sem,
            recv_sem=frecv_sem,
            device_id=jpeer(k),
            device_id_type=MESH,
        ).start()

    ring_step(1)
    ring_step(2)

    whole = fbuf_ref
    pltpu.make_async_copy(whole, whole, frecv_sem).wait()
    total = fsend_ref[j].astype(jnp.float32)
    for k in range(NJ - 1):
        total = total + fbuf_ref[k].astype(jnp.float32)
    unit_grad = jnp.concatenate([total[:FROWS], total[FROWS:]], axis=1)
    mine = pl.ds(pl.multiple_of(j * FROWS, FROWS), FROWS)
    unit = zfull_ref[mine, :]
    along = jnp.sum(unit * unit_grad, axis=1, keepdims=True)
    length = zlen_ref[mine, :]
    rows = unit_grad - unit * along
    gsend_ref[...] = jnp.concatenate([rows[:, :LANES] / length, rows[:, LANES:] / length], axis=0).astype(jnp.bfloat16)
    for k in range(1, NJ):
        pltpu.make_async_remote_copy(
            src_ref=gsend_ref,
            dst_ref=gbuf_ref.at[j],
            send_sem=gsend_sem,
            recv_sem=grecv_sem,
            device_id=jpeer(k),
            device_id_type=MESH,
        ).start()
    gbuf_ref[j] = gsend_ref[...]

    for step in range(3, STEPS):
        ring_step(step)

    got = gbuf_ref.at[pl.ds(0, NJ - 1)]
    pltpu.make_async_copy(got, got, grecv_sem).wait()
    for i in range(NJ // 2):
        one = gbuf_ref[2 * i].astype(jnp.float32)
        two = gbuf_ref[2 * i + 1].astype(jnp.float32)
        left = jnp.concatenate([one[:FROWS], two[:FROWS]], axis=0)
        right = jnp.concatenate([one[FROWS:], two[FROWS:]], axis=0)
        fout_ref[2 * FROWS * i:2 * FROWS * (i + 1), :] = jnp.concatenate([left, right], axis=1).astype(jnp.bfloat16)

    for sub in range(SUBS):
        at = pl.ds(sub * SUB, SUB)
        total = chunk(0, sub)[...].astype(jnp.float32)
        for way in range(2):
            ring_copy(way, STEPS - 1, sub).wait_recv()
            total = total + ring_ref[way, STEPS - 1, :, at].astype(jnp.float32)
        wout_ref[:, at] = total.astype(jnp.bfloat16)

    for it in range(ITERS):
        whole = pbuf_ref.at[it]
        pltpu.make_async_copy(whole, whole, psend_sem.at[it]).wait()
        got = cbuf_ref.at[it]
        pltpu.make_async_copy(got, got, csend_sem.at[it]).wait()
    pltpu.make_async_copy(sbuf_ref, sbuf_ref, ssend_sem).wait()
    pltpu.make_async_copy(fbuf_ref, fbuf_ref, fsend_sem).wait()
    pltpu.make_async_copy(fbuf_ref, fbuf_ref, gsend_sem).wait()
    for step in range(STEPS):
        for way in range(2):
            for sub in subs_of(way, step):
                ring_copy(way, step, sub).wait_send()


def shards(teacher_feats, student_feats, teacher_weight, student_weight):
    f32, bf16 = jnp.float32, jnp.bfloat16
    vmem, dma = pltpu.VMEM, pltpu.SemaphoreType.DMA
    scratch = [
        vmem((B, D), bf16),
        vmem((B, D), bf16),
        vmem((D, C), bf16),
        vmem((D, C), bf16),
        vmem((TILES, B, LANES), f32),
        vmem((TILES, B, LANES), f32),
        vmem((D, C), bf16),
        vmem((B, C), bf16),
        vmem((D, C), bf16),
        vmem((2, STEPS, ROWS, C), bf16),
        vmem((B, D), bf16),
        vmem((B, D), bf16),
        vmem((D, B), bf16),
        vmem((B, D), f32),
        vmem((B, LANES), f32),
        vmem((WTILES, 1, WIDE), f32),
        vmem((WTILES, WIDE), f32),
        vmem((ITERS, WTILES, WIDE), bf16),
        vmem((ITERS, NZ - 1, WTILES, WIDE), bf16),
        vmem((WTILES, 1, WIDE), f32),
        vmem((B, LANES), f32),
        vmem((B, LANES), f32),
        vmem((ITERS, 1, B), f32),
        vmem((ITERS, NJ - 1, 1, B), f32),
        vmem((1, B), f32),
        vmem((NJ - 1, 1, B), f32),
        vmem((NJ, 2 * FROWS, LANES), bf16),
        vmem((NJ - 1, 2 * FROWS, LANES), bf16),
        vmem((2 * FROWS, LANES), bf16),
        vmem((NJ, 2 * FROWS, LANES), bf16),
        dma((ITERS,)), dma((ITERS,)), dma((ITERS,)), dma((ITERS,)), dma, dma,
        dma, dma, dma, dma, dma((2, STEPS, SUBS)), dma((2, STEPS, SUBS)), dma((3,)), dma((PARTS,)),
    ]
    return pl.pallas_call(
        kernel,
        out_shape=(jax.ShapeDtypeStruct((ROWS, C), bf16), jax.ShapeDtypeStruct((B, D), bf16)),
        in_specs=[pl.BlockSpec(memory_space=pltpu.HBM)] * 4,
        out_specs=(pl.BlockSpec(memory_space=pltpu.VMEM), pl.BlockSpec(memory_space=pltpu.VMEM)),
        scratch_shapes=scratch,
        compiler_params=pltpu.CompilerParams(
            collective_id=0, has_side_effects=True, vmem_limit_bytes=(536 << 20) // 10
        ),
        cost_estimate=pl.CostEstimate(
            flops=8 * B * C * D, bytes_accessed=4 * D * C + 6 * B * D, transcendentals=2 * B * C
        ),
    )(teacher_feats, student_feats, teacher_weight, student_weight)


def solution(mesh):
    return jax.shard_map(
        shards,
        mesh=mesh,
        in_specs=(P("batch", None), P("batch", None), P(None, "proto"), P(None, "proto")),
        out_specs=(P("batch", "proto"), P("batch", None)),
        check_vma=False,
    )
```

```python
import functools
import math

import jax
import jax.numpy as jnp
from jax import lax
from jax.experimental import pallas as pl
from jax.experimental.pallas import tpu as pltpu
from jax.sharding import PartitionSpec as P

ITERS = 3
TEACHER_TEMP = 0.07
STUDENT_TEMP = 0.1
EPSILON = 1e-06
MESH = pl.DeviceIdType.MESH

NZ = 16
NJ = 32
D = 256
B = 256
C = 4096
PROTOS = C * NJ
CROPS = B * NZ
LANES = 128
TILES = C // LANES
WIDE = 256
WTILES = C // WIDE
PARTS = 4
PART = C // PARTS
ROWS = D // NZ
NX, NY = 4, 4
HALF = NZ // 2
EARLY = 2
FROWS = B // NJ
Z_ORDER = sorted(range(1, NZ), key=lambda k: -min(k, NZ - k))


def kernel(
    tf_hbm, sf_hbm, tw_hbm, sw_hbm, wout_ref, fout_ref,
    tf_ref, sf_ref, tw_ref, sw_ref,
    e_ref, s_ref, ws_ref, grad_ref, all_ref, we_ref, wsx_ref,
    zt_ref, zs_ref, zfull_ref, zlen_ref,
    twt_ref, swt_ref, tscale_ref, wacc_ref, wsend_ref, wrecv_ref, xsend_ref, xbuf_ref,
    pr_ref, pf_ref, psend_ref, pbuf_ref, u_ref, crep_ref, srep_ref,
    csend_ref, cbuf_ref, ssend_ref, sbuf_ref,
    fsend_ref, fbuf_ref, gsend_ref, gbuf_ref,
    psend_sem, precv_sem, csend_sem, crecv_sem, ssend_sem, srecv_sem,
    fsend_sem, frecv_sem, gsend_sem, grecv_sem, load_sem, tload_sem,
    gather_send, gather_recv, xsend_sem, xrecv_sem, wsend_sem, wrecv_sem,
):
    z = lax.axis_index("batch")
    j = lax.axis_index("proto")

    def zpeer(k):
        return (lax.rem(z + k, NZ), j)

    def jpeer(k):
        return (z, lax.rem(j + k, NJ))

    core = lax.rem(j, 2)
    x = lax.rem(j // 2, NX)
    y = j // (2 * NX)

    def xpeer(k):
        return (z, (y * NX + lax.rem(x + k, NX)) * 2 + core)

    def ypeer(k):
        return (z, (lax.rem(y + k, NY) * NX + x) * 2 + core)

    barrier = pltpu.get_barrier_semaphore()
    for k in range(1, NJ):
        pl.semaphore_signal(barrier, 1, device_id=jpeer(k), device_id_type=MESH)
    for k in Z_ORDER:
        pl.semaphore_signal(barrier, 1, device_id=zpeer(k), device_id_type=MESH)

    load_tf = pltpu.make_async_copy(tf_hbm, tf_ref, load_sem.at[0])
    load_sf = pltpu.make_async_copy(sf_hbm, sf_ref, load_sem.at[1])
    load_sw = pltpu.make_async_copy(sw_hbm, sw_ref, load_sem.at[2])

    def load_tw(part):
        at = pl.ds(pl.multiple_of(part * PART, PART), PART)
        return pltpu.make_async_copy(tw_hbm.at[:, at], tw_ref.at[:, at], tload_sem.at[part])

    load_tf.start()
    for part in range(PARTS):
        load_tw(part).start()
    load_sf.start()
    load_sw.start()
    load_tf.wait()

    tf = tf_ref[...].astype(jnp.float32)
    zt_ref[...] = (tf * lax.rsqrt(jnp.sum(tf * tf, axis=1, keepdims=True) + EPSILON)).astype(jnp.bfloat16)

    def columns(t):
        return pl.ds(pl.multiple_of(t * WIDE, WIDE), WIDE)

    def inverse_lengths(values):
        return lax.rsqrt(jnp.sum(values * values, axis=0, keepdims=True) + EPSILON)

    def teacher_tile(t, carry):
        raw = tw_ref[:, columns(t)]
        scale = inverse_lengths(raw.astype(jnp.float32)) * (1.0 / TEACHER_TEMP)
        dots = jnp.dot(zt_ref[...], raw, preferred_element_type=jnp.float32)
        e = jnp.exp(dots * scale)
        e_ref[2 * t] = e[:, :LANES]
        e_ref[2 * t + 1] = e[:, LANES:]
        pr_ref[t] = jnp.sum(e, axis=0, keepdims=True)
        return carry

    for part in range(PARTS):
        load_tw(part).wait()
        lax.fori_loop(part * (WTILES // PARTS), (part + 1) * (WTILES // PARTS), teacher_tile, 0, unroll=True)

    def send_protos(it):
        pf_ref[...] = jnp.concatenate([pr_ref[t] for t in range(WTILES)], axis=0)
        psend_ref[it] = pf_ref[...].astype(jnp.bfloat16)
        for k in Z_ORDER:
            pltpu.make_async_remote_copy(
                src_ref=psend_ref.at[it],
                dst_ref=pbuf_ref.at[it, k - 1],
                send_sem=psend_sem.at[it],
                recv_sem=precv_sem.at[it],
                device_id=zpeer(k),
                device_id_type=MESH,
            ).start()

    def receive_protos(it):
        whole = pbuf_ref.at[it]
        pltpu.make_async_copy(whole, whole, precv_sem.at[it]).wait()
        total = pf_ref[...]
        for k in range(NZ - 1):
            total = total + pbuf_ref[it, k].astype(jnp.float32)
        scale = 1.0 / total
        for t in range(WTILES):
            u_ref[t] = scale[t:t + 1]

    pl.semaphore_wait(barrier, NJ + NZ - 2)
    send_protos(0)

    load_sf.wait()
    load_sw.wait()
    sf = sf_ref[...].astype(jnp.float32)
    slen = jnp.sqrt(jnp.sum(sf * sf, axis=1, keepdims=True) + EPSILON)
    sfull = sf / slen
    zfull_ref[...] = sfull
    zlen_ref[...] = jnp.broadcast_to(slen, (B, LANES))
    zs_ref[...] = sfull.astype(jnp.bfloat16)

    def student_tile(t, acc):
        values = sw_ref[:, columns(t)].astype(jnp.float32)
        ws = (values * inverse_lengths(values)).astype(jnp.bfloat16)
        ws_ref[:, columns(t)] = ws
        dots = jnp.dot(zs_ref[...], ws, preferred_element_type=jnp.float32)
        s = jnp.exp(dots * (1.0 / STUDENT_TEMP))
        s_ref[2 * t] = s[:, :LANES]
        s_ref[2 * t + 1] = s[:, LANES:]
        return acc + s[:, :LANES] + s[:, LANES:]

    sacc = lax.fori_loop(0, WTILES, student_tile, jnp.zeros((B, LANES), jnp.float32), unroll=2)
    ssend_ref[...] = jnp.sum(jnp.transpose(sacc), axis=0, keepdims=True)
    for k in range(1, NJ):
        pltpu.make_async_remote_copy(
            src_ref=ssend_ref,
            dst_ref=sbuf_ref.at[k - 1],
            send_sem=ssend_sem,
            recv_sem=srecv_sem,
            device_id=jpeer(k),
            device_id_type=MESH,
        ).start()

    def post(src, dst, stage, peer):
        pltpu.make_async_remote_copy(
            src_ref=src,
            dst_ref=dst,
            send_sem=gather_send.at[stage],
            recv_sem=gather_recv.at[stage],
            device_id=peer,
            device_id_type=MESH,
        ).start()

    def arrived(stage, amount):
        pltpu.make_async_copy(amount, amount, gather_recv.at[stage]).wait()

    amounts = (
        all_ref.at[0, pl.ds(0, NZ - 1), 0, 0],
        all_ref.at[0, pl.ds(0, HALF), 0, pl.ds(0, NX - 1)],
        all_ref.at[0, pl.ds(0, HALF), 0, pl.ds(0, NX - 1)],
        all_ref.at[0, pl.ds(0, EARLY), pl.ds(0, NY - 1)],
        all_ref.at[0, pl.ds(0, EARLY), pl.ds(0, NY - 1)],
        all_ref.at[0, pl.ds(0, HALF - EARLY), pl.ds(0, NY - 1)],
        all_ref.at[0, pl.ds(0, HALF - EARLY), pl.ds(0, NY - 1)],
        all_ref.at[0],
    )
    first, second = pl.ds(0, HALF), pl.ds(HALF, HALF)

    def gather_z():
        rows = pl.ds(pl.multiple_of((j // 2) * ROWS, ROWS), ROWS)
        both = jnp.where(core == 0, zt_ref[rows, :].astype(jnp.float32), zs_ref[rows, :].astype(jnp.float32))
        all_ref[core, z, y, x] = both.astype(jnp.bfloat16)
        mine = all_ref.at[core, z, y, x]
        for k in Z_ORDER:
            post(mine, mine, 0, zpeer(k))

    def gather_one():
        arrived(0, amounts[0])
        for k in (2, 1, 3):
            one = all_ref.at[core, first, y, x]
            post(one, one, 1, xpeer(k))
            two = all_ref.at[core, second, y, x]
            post(two, two, 2, ypeer(k))

    def gather_two(begin, end, stage):
        for k in (2, 1, 3):
            one = all_ref.at[core, pl.ds(begin, end - begin), y]
            post(one, one, stage, ypeer(k))
            two = all_ref.at[core, pl.ds(HALF + begin, end - begin), :, x]
            post(two, two, stage + 1, xpeer(k))

    def gather_core():
        mine = all_ref.at[core]
        post(mine, mine, 7, (z, j + 1 - 2 * core))

    gather_z()

    for it in range(ITERS):
        if it > 0:
            def proto_tiles(g, carry):
                totals = [None] * 4
                for r in range(0, B, 8):
                    c = crep_ref[r:r + 8]
                    for i in range(4):
                        term = e_ref[4 * g + i, r:r + 8] * c
                        totals[i] = term if r == 0 else totals[i] + term
                for i in range(4):
                    pr_ref[2 * g + i // 2, :, (i % 2) * LANES:(i % 2 + 1) * LANES] = jnp.sum(
                        totals[i], axis=0, keepdims=True
                    )
                return carry

            lax.fori_loop(0, TILES // 4, proto_tiles, 0, unroll=2)
            send_protos(it)
        if it == 1:
            gather_one()
            own = columns(z)
            raw = jnp.transpose(tw_ref[:, own].astype(jnp.float32))
            twt_ref[...] = raw.astype(jnp.bfloat16)
            scale = lax.rsqrt(jnp.sum(raw * raw, axis=1, keepdims=True) + EPSILON) * (1.0 / TEACHER_TEMP)
            tscale_ref[...] = jnp.broadcast_to(scale, (WIDE, LANES))
            swt_ref[...] = jnp.transpose(ws_ref[:, own].astype(jnp.float32)).astype(jnp.bfloat16)
            arrived(1, amounts[1])
            arrived(2, amounts[2])
            gather_two(0, EARLY, 3)
        if it == 2:
            arrived(3, amounts[3])
            arrived(4, amounts[4])
            gather_two(EARLY, HALF, 5)
        receive_protos(it)
        last = it == ITERS - 1

        def crop_tile(t, acc):
            for h in range(2):
                scaled = e_ref[2 * t + h] * u_ref[t, :, h * LANES:(h + 1) * LANES]
                if last:
                    e_ref[2 * t + h] = scaled
                acc = acc + scaled
            return acc

        acc = lax.fori_loop(0, WTILES, crop_tile, jnp.zeros((B, LANES), jnp.float32), unroll=4)
        row = jnp.sum(jnp.transpose(acc), axis=0, keepdims=True)
        csend_ref[it] = row
        for k in range(1, NJ):
            pltpu.make_async_remote_copy(
                src_ref=csend_ref.at[it],
                dst_ref=cbuf_ref.at[it, k - 1],
                send_sem=csend_sem.at[it],
                recv_sem=crecv_sem.at[it],
                device_id=jpeer(k),
                device_id_type=MESH,
            ).start()
        if last:
            arrived(5, amounts[5])
            arrived(6, amounts[6])
            gather_core()
        got = cbuf_ref.at[it]
        pltpu.make_async_copy(got, got, crecv_sem.at[it]).wait()
        for k in range(NJ - 1):
            row = row + cbuf_ref[it, k]
        crop_scale = 1.0 / row
        if last:
            crop_scale = crop_scale * float(PROTOS)
            xsend_ref[:, :B] = crop_scale
        crep_ref[...] = jnp.transpose(jnp.broadcast_to(crop_scale, (LANES, B)))

    pltpu.make_async_copy(sbuf_ref, sbuf_ref, srecv_sem).wait()
    row = ssend_ref[...]
    for k in range(NJ - 1):
        row = row + sbuf_ref[k]
    inverse = float(PROTOS) / row
    xsend_ref[:, B:] = inverse
    for k in Z_ORDER:
        pltpu.make_async_remote_copy(
            src_ref=xsend_ref,
            dst_ref=xbuf_ref.at[k - 1],
            send_sem=xsend_sem,
            recv_sem=xrecv_sem.at[k - 1],
            device_id=zpeer(k),
            device_id_type=MESH,
        ).start()
    srep_ref[...] = jnp.transpose(jnp.broadcast_to(inverse, (LANES, B)))
    weight_factor = math.sqrt(D / CROPS)
    feature_factor = math.sqrt(D / PROTOS)

    def grad_tile(t, carry):
        c = crep_ref[...]
        halves = [s_ref[2 * t + h] * srep_ref[...] - e_ref[2 * t + h] * c for h in range(2)]
        grad = jnp.concatenate([half.astype(jnp.bfloat16) for half in halves], axis=1)
        grad_ref[:, columns(t)] = grad
        return carry

    lax.fori_loop(0, WTILES, grad_tile, 0, unroll=4)

    feature = lax.dot_general(
        grad_ref[...], ws_ref[...], (((1,), (1,)), ((), ())), preferred_element_type=jnp.float32
    ) * feature_factor
    for i in range(NJ):
        rows = feature[i * FROWS:(i + 1) * FROWS]
        fsend_ref[i] = jnp.concatenate([rows[:, :LANES], rows[:, LANES:]], axis=0).astype(jnp.bfloat16)
    for k in range(1, NJ):
        pltpu.make_async_remote_copy(
            src_ref=fsend_ref.at[lax.rem(j + k, NJ)],
            dst_ref=fbuf_ref.at[k - 1],
            send_sem=fsend_sem,
            recv_sem=frecv_sem,
            device_id=jpeer(k),
            device_id_type=MESH,
        ).start()

    arrived(7, amounts[7])
    ucol = jnp.transpose(jnp.broadcast_to(u_ref[z], (LANES, WIDE)))

    def own_tile(b, carry):
        zt = all_ref[0, b].reshape(B, D)
        zs = all_ref[1, b].reshape(B, D)
        contract = (((1,), (1,)), ((), ()))
        dots = lax.dot_general(twt_ref[...], zt, contract, preferred_element_type=jnp.float32)
        logits = lax.dot_general(swt_ref[...], zs, contract, preferred_element_type=jnp.float32)
        for h in range(2):
            at = slice(h * LANES, (h + 1) * LANES)
            we_ref[b, :, at] = jnp.exp(dots[:, at] * tscale_ref[...]) * ucol
        wsx_ref[b] = jnp.exp(logits * (1.0 / STUDENT_TEMP))
        return carry

    lax.fori_loop(0, NZ, own_tile, 0, unroll=2)

    def block(b, scales):
        grad = (wsx_ref[b] * scales[:, B:] - we_ref[b] * scales[:, :B]).astype(jnp.bfloat16)
        return jnp.dot(grad, all_ref[1, b].reshape(B, D), preferred_element_type=jnp.float32)

    wacc_ref[...] = block(z, xsend_ref[...])
    for k in reversed(Z_ORDER):
        slot = xbuf_ref.at[k - 1]
        pltpu.make_async_copy(slot, slot, xrecv_sem.at[k - 1]).wait()
        wacc_ref[...] += block(lax.rem(z + NZ - k, NZ), xbuf_ref[k - 1])
    weight = (jnp.transpose(wacc_ref[...]) * weight_factor).astype(jnp.bfloat16)
    for b in range(NZ):
        wsend_ref[b] = weight[b * ROWS:(b + 1) * ROWS]
    for k in Z_ORDER:
        pltpu.make_async_remote_copy(
            src_ref=wsend_ref.at[lax.rem(z + k, NZ)],
            dst_ref=wrecv_ref.at[k - 1],
            send_sem=wsend_sem,
            recv_sem=wrecv_sem,
            device_id=zpeer(k),
            device_id_type=MESH,
        ).start()

    whole = fbuf_ref
    pltpu.make_async_copy(whole, whole, frecv_sem).wait()
    total = fsend_ref[j].astype(jnp.float32)
    for k in range(NJ - 1):
        total = total + fbuf_ref[k].astype(jnp.float32)
    unit_grad = jnp.concatenate([total[:FROWS], total[FROWS:]], axis=1)
    mine = pl.ds(pl.multiple_of(j * FROWS, FROWS), FROWS)
    unit = zfull_ref[mine, :]
    along = jnp.sum(unit * unit_grad, axis=1, keepdims=True)
    length = zlen_ref[mine, :]
    rows = unit_grad - unit * along
    gsend_ref[...] = jnp.concatenate([rows[:, :LANES] / length, rows[:, LANES:] / length], axis=0).astype(jnp.bfloat16)
    for k in range(1, NJ):
        pltpu.make_async_remote_copy(
            src_ref=gsend_ref,
            dst_ref=gbuf_ref.at[j],
            send_sem=gsend_sem,
            recv_sem=grecv_sem,
            device_id=jpeer(k),
            device_id_type=MESH,
        ).start()
    gbuf_ref[j] = gsend_ref[...]

    got = gbuf_ref.at[pl.ds(0, NJ - 1)]
    pltpu.make_async_copy(got, got, grecv_sem).wait()
    for i in range(NJ // 2):
        one = gbuf_ref[2 * i].astype(jnp.float32)
        two = gbuf_ref[2 * i + 1].astype(jnp.float32)
        left = jnp.concatenate([one[:FROWS], two[:FROWS]], axis=0)
        right = jnp.concatenate([one[FROWS:], two[FROWS:]], axis=0)
        fout_ref[2 * FROWS * i:2 * FROWS * (i + 1), :] = jnp.concatenate([left, right], axis=1).astype(jnp.bfloat16)

    pltpu.make_async_copy(wrecv_ref, wrecv_ref, wrecv_sem).wait()
    wout_ref[:, columns(z)] = wsend_ref[z]
    for k in range(1, NZ):
        wout_ref[:, columns(lax.rem(z + NZ - k, NZ))] = wrecv_ref[k - 1]

    for it in range(ITERS):
        whole = pbuf_ref.at[it]
        pltpu.make_async_copy(whole, whole, psend_sem.at[it]).wait()
        got = cbuf_ref.at[it]
        pltpu.make_async_copy(got, got, csend_sem.at[it]).wait()
    pltpu.make_async_copy(sbuf_ref, sbuf_ref, ssend_sem).wait()
    pltpu.make_async_copy(fbuf_ref, fbuf_ref, fsend_sem).wait()
    pltpu.make_async_copy(fbuf_ref, fbuf_ref, gsend_sem).wait()
    pltpu.make_async_copy(xbuf_ref, xbuf_ref, xsend_sem).wait()
    pltpu.make_async_copy(wrecv_ref, wrecv_ref, wsend_sem).wait()
    for stage in range(len(amounts)):
        pltpu.make_async_copy(amounts[stage], amounts[stage], gather_send.at[stage]).wait()


def shards(teacher_feats, student_feats, teacher_weight, student_weight):
    f32, bf16 = jnp.float32, jnp.bfloat16
    vmem, dma = pltpu.VMEM, pltpu.SemaphoreType.DMA
    scratch = [
        vmem((B, D), bf16),
        vmem((B, D), bf16),
        vmem((D, C), bf16),
        vmem((D, C), bf16),
        vmem((TILES, B, LANES), f32),
        vmem((TILES, B, LANES), f32),
        vmem((D, C), bf16),
        vmem((B, C), bf16),
        vmem((2, NZ, NY, NX, ROWS, D), bf16),
        vmem((NZ, WIDE, B), f32),
        vmem((NZ, WIDE, B), f32),
        vmem((B, D), bf16),
        vmem((B, D), bf16),
        vmem((B, D), f32),
        vmem((B, LANES), f32),
        vmem((WIDE, D), bf16),
        vmem((WIDE, D), bf16),
        vmem((WIDE, LANES), f32),
        vmem((WIDE, D), f32),
        vmem((NZ, ROWS, WIDE), bf16),
        vmem((NZ - 1, ROWS, WIDE), bf16),
        vmem((1, 2 * B), f32),
        vmem((NZ - 1, 1, 2 * B), f32),
        vmem((WTILES, 1, WIDE), f32),
        vmem((WTILES, WIDE), f32),
        vmem((ITERS, WTILES, WIDE), bf16),
        vmem((ITERS, NZ - 1, WTILES, WIDE), bf16),
        vmem((WTILES, 1, WIDE), f32),
        vmem((B, LANES), f32),
        vmem((B, LANES), f32),
        vmem((ITERS, 1, B), f32),
        vmem((ITERS, NJ - 1, 1, B), f32),
        vmem((1, B), f32),
        vmem((NJ - 1, 1, B), f32),
        vmem((NJ, 2 * FROWS, LANES), bf16),
        vmem((NJ - 1, 2 * FROWS, LANES), bf16),
        vmem((2 * FROWS, LANES), bf16),
        vmem((NJ, 2 * FROWS, LANES), bf16),
        dma((ITERS,)), dma((ITERS,)), dma((ITERS,)), dma((ITERS,)), dma, dma,
        dma, dma, dma, dma, dma((3,)), dma((PARTS,)),
        dma((8,)), dma((8,)), dma, dma((NZ - 1,)), dma, dma,
    ]
    return pl.pallas_call(
        kernel,
        out_shape=(jax.ShapeDtypeStruct((ROWS, C), bf16), jax.ShapeDtypeStruct((B, D), bf16)),
        in_specs=[pl.BlockSpec(memory_space=pltpu.HBM)] * 4,
        out_specs=(pl.BlockSpec(memory_space=pltpu.VMEM), pl.BlockSpec(memory_space=pltpu.VMEM)),
        scratch_shapes=scratch,
        compiler_params=pltpu.CompilerParams(
            collective_id=0, has_side_effects=True, vmem_limit_bytes=(536 << 20) // 10
        ),
        cost_estimate=pl.CostEstimate(
            flops=8 * B * C * D, bytes_accessed=4 * D * C + 6 * B * D, transcendentals=2 * B * C
        ),
    )(teacher_feats, student_feats, teacher_weight, student_weight)


def solution(mesh):
    return jax.shard_map(
        shards,
        mesh=mesh,
        in_specs=(P("batch", None), P("batch", None), P(None, "proto"), P(None, "proto")),
        out_specs=(P("batch", "proto"), P("batch", None)),
        check_vma=False,
    )
```

```python
import functools
import math

import jax
import jax.numpy as jnp
from jax import lax
from jax.experimental import pallas as pl
from jax.experimental.pallas import tpu as pltpu
from jax.sharding import PartitionSpec as P

ITERS = 3
TEACHER_TEMP = 0.07
STUDENT_TEMP = 0.1
EPSILON = 1e-06
MESH = pl.DeviceIdType.MESH

NZ = 16
NJ = 32
D = 256
B = 256
C = 4096
PROTOS = C * NJ
CROPS = B * NZ
LANES = 128
TILES = C // LANES
HTILES = TILES // 2
WIDE = 256
WTILES = C // WIDE
PARTS = 4
PART = C // PARTS
ROWS = D // NZ
NX, NY = 4, 4
HALF = NZ // 2
EARLY = 3
FROWS = B // NJ
Z_ORDER = sorted(range(1, NZ), key=lambda k: -min(k, NZ - k))


def kernel(
    tf_hbm, sf_hbm, tw_hbm, sw_hbm, wout_ref, fout_ref,
    tf_ref, sf_ref, tw_ref, sw_ref,
    e_ref, s_ref, ws_ref, grad_ref, all_ref, we_ref, wsx_ref,
    zt_ref, zs_ref, ztt_ref, zst_ref, zfull_ref, zlen_ref,
    twt_ref, swt_ref, tscale_ref, ucol_ref, wacc_ref, wsend_ref, wrecv_ref, xsend_ref, xbuf_ref,
    pr_ref, pf_ref, psend_ref, pbuf_ref, u_ref, crep_ref, srep_ref,
    csend_ref, cbuf_ref, ssend_ref, sbuf_ref,
    fsend_ref, fbuf_ref, gsend_ref, gbuf_ref,
    psend_sem, precv_sem, csend_sem, crecv_sem, ssend_sem, srecv_sem,
    fsend_sem, frecv_sem, gsend_sem, grecv_sem, load_sem, tload_sem,
    gather_send, gather_recv, xsend_sem, xrecv_sem, wsend_sem, wrecv_sem,
):
    z = lax.axis_index("batch")
    j = lax.axis_index("proto")

    def zpeer(k):
        return (lax.rem(z + k, NZ), j)

    def jpeer(k):
        return (z, lax.rem(j + k, NJ))

    core = lax.rem(j, 2)
    x = lax.rem(j // 2, NX)
    y = j // (2 * NX)

    def xpeer(k):
        return (z, (y * NX + lax.rem(x + k, NX)) * 2 + core)

    def ypeer(k):
        return (z, (lax.rem(y + k, NY) * NX + x) * 2 + core)

    barrier = pltpu.get_barrier_semaphore()
    for k in Z_ORDER:
        pl.semaphore_signal(barrier, 1, device_id=zpeer(k), device_id_type=MESH)
    for k in range(1, NJ):
        pl.semaphore_signal(barrier, 1, device_id=jpeer(k), device_id_type=MESH)

    load_tf = pltpu.make_async_copy(tf_hbm, tf_ref, load_sem.at[0])
    load_sf = pltpu.make_async_copy(sf_hbm, sf_ref, load_sem.at[1])
    load_sw = pltpu.make_async_copy(sw_hbm, sw_ref, load_sem.at[2])

    def load_tw(part):
        at = pl.ds(pl.multiple_of(part * PART, PART), PART)
        return pltpu.make_async_copy(tw_hbm.at[:, at], tw_ref.at[:, at], tload_sem.at[part])

    load_tf.start()
    for part in range(PARTS):
        load_tw(part).start()
    load_sf.start()
    load_sw.start()
    load_tf.wait()

    tf = tf_ref[...].astype(jnp.float32)
    zt_ref[...] = (tf * lax.rsqrt(jnp.sum(tf * tf, axis=1, keepdims=True) + EPSILON)).astype(jnp.bfloat16)

    def columns(t):
        return pl.ds(pl.multiple_of(t * WIDE, WIDE), WIDE)

    def inverse_lengths(values):
        return lax.rsqrt(jnp.sum(values * values, axis=0, keepdims=True) + EPSILON)

    def teacher_tile(t, carry):
        raw = tw_ref[:, columns(t)]
        scale = inverse_lengths(raw.astype(jnp.float32)) * (1.0 / TEACHER_TEMP)
        dots = jnp.dot(zt_ref[...], raw, preferred_element_type=jnp.float32)
        e = jnp.exp(dots * scale)
        e_ref[2 * t] = e[:, :LANES]
        e_ref[2 * t + 1] = e[:, LANES:]
        sums = jnp.sum(e, axis=0, keepdims=True)
        pr_ref[2 * t] = sums[:, :LANES]
        pr_ref[2 * t + 1] = sums[:, LANES:]
        return carry

    for part in range(PARTS):
        load_tw(part).wait()
        lax.fori_loop(part * (WTILES // PARTS), (part + 1) * (WTILES // PARTS), teacher_tile, 0, unroll=True)

    def send_protos(it):
        for part in range(2):
            sums = jnp.concatenate([pr_ref[part * HTILES + t] for t in range(HTILES)], axis=0)
            pf_ref[part] = sums
            psend_ref[it, part] = sums.astype(jnp.bfloat16)
        for k in Z_ORDER:
            for part in range(2):
                pltpu.make_async_remote_copy(
                    src_ref=psend_ref.at[it, part],
                    dst_ref=pbuf_ref.at[it, part, k - 1],
                    send_sem=psend_sem.at[it, part],
                    recv_sem=precv_sem.at[it, part],
                    device_id=zpeer(k),
                    device_id_type=MESH,
                ).start()

    def receive_protos(it, part):
        whole = pbuf_ref.at[it, part]
        pltpu.make_async_copy(whole, whole, precv_sem.at[it, part]).wait()
        total = pf_ref[part]
        for k in range(NZ - 1):
            total = total + pbuf_ref[it, part, k].astype(jnp.float32)
        scale = 1.0 / total
        for t in range(HTILES):
            u_ref[part * HTILES + t] = scale[t:t + 1]

    pl.semaphore_wait(barrier, NJ + NZ - 2)
    send_protos(0)

    load_sf.wait()
    load_sw.wait()
    sf = sf_ref[...].astype(jnp.float32)
    slen = jnp.sqrt(jnp.sum(sf * sf, axis=1, keepdims=True) + EPSILON)
    sfull = sf / slen
    zfull_ref[...] = sfull
    zlen_ref[...] = jnp.broadcast_to(slen, (B, LANES))
    zs_ref[...] = sfull.astype(jnp.bfloat16)

    def student_tile(t, acc):
        values = sw_ref[:, columns(t)].astype(jnp.float32)
        ws = (values * inverse_lengths(values)).astype(jnp.bfloat16)
        ws_ref[:, columns(t)] = ws
        dots = jnp.dot(zs_ref[...], ws, preferred_element_type=jnp.float32)
        s = jnp.exp(dots * (1.0 / STUDENT_TEMP))
        s_ref[2 * t] = s[:, :LANES]
        s_ref[2 * t + 1] = s[:, LANES:]
        return acc + s[:, :LANES] + s[:, LANES:]

    sacc = lax.fori_loop(0, WTILES, student_tile, jnp.zeros((B, LANES), jnp.float32), unroll=2)
    ssend_ref[...] = jnp.sum(jnp.transpose(sacc), axis=0, keepdims=True)
    for k in range(1, NJ):
        pltpu.make_async_remote_copy(
            src_ref=ssend_ref,
            dst_ref=sbuf_ref.at[k - 1],
            send_sem=ssend_sem,
            recv_sem=srecv_sem,
            device_id=jpeer(k),
            device_id_type=MESH,
        ).start()

    def post(src, dst, stage, peer):
        pltpu.make_async_remote_copy(
            src_ref=src,
            dst_ref=dst,
            send_sem=gather_send.at[stage],
            recv_sem=gather_recv.at[stage],
            device_id=peer,
            device_id_type=MESH,
        ).start()

    def arrived(stage, amount):
        pltpu.make_async_copy(amount, amount, gather_recv.at[stage]).wait()

    amounts = (
        all_ref.at[0, pl.ds(0, NZ - 1), 0, 0],
        all_ref.at[0, pl.ds(0, HALF), 0, pl.ds(0, NX - 1)],
        all_ref.at[0, pl.ds(0, HALF), 0, pl.ds(0, NX - 1)],
        all_ref.at[0, pl.ds(0, EARLY), pl.ds(0, NY - 1)],
        all_ref.at[0, pl.ds(0, EARLY), pl.ds(0, NY - 1)],
        all_ref.at[0, pl.ds(0, HALF - EARLY), pl.ds(0, NY - 1)],
        all_ref.at[0, pl.ds(0, HALF - EARLY), pl.ds(0, NY - 1)],
        all_ref.at[0, pl.ds(0, EARLY)],
        all_ref.at[0, pl.ds(0, EARLY)],
        all_ref.at[0, pl.ds(0, HALF - EARLY)],
        all_ref.at[0, pl.ds(0, HALF - EARLY)],
    )
    first, second = pl.ds(0, HALF), pl.ds(HALF, HALF)

    def gather_z():
        rows = pl.ds(pl.multiple_of((j // 2) * ROWS, ROWS), ROWS)
        ztt_ref[...] = jnp.transpose(zt_ref[...].astype(jnp.float32))
        zst_ref[...] = jnp.transpose(zs_ref[...].astype(jnp.float32))
        all_ref[core, z, y, x] = jnp.where(core == 0, ztt_ref[rows, :], zst_ref[rows, :]).astype(jnp.bfloat16)
        mine = all_ref.at[core, z, y, x]
        for k in Z_ORDER:
            post(mine, mine, 0, zpeer(k))

    def gather_one():
        arrived(0, amounts[0])
        for k in (2, 1, 3):
            one = all_ref.at[core, first, y, x]
            post(one, one, 1, xpeer(k))
            two = all_ref.at[core, second, y, x]
            post(two, two, 2, ypeer(k))

    def gather_two(begin, end, stage):
        for k in (2, 1, 3):
            one = all_ref.at[core, pl.ds(begin, end - begin), y]
            post(one, one, stage, ypeer(k))
            two = all_ref.at[core, pl.ds(HALF + begin, end - begin), :, x]
            post(two, two, stage + 1, xpeer(k))

    def gather_core(begin, end, stage):
        for half in range(2):
            mine = all_ref.at[core, pl.ds(half * HALF + begin, end - begin)]
            post(mine, mine, stage + half, (z, j + 1 - 2 * core))

    def own_tile(b):
        dots = jnp.dot(twt_ref[...], all_ref[0, b].reshape(D, B), preferred_element_type=jnp.float32)
        logits = jnp.dot(swt_ref[...], all_ref[1, b].reshape(D, B), preferred_element_type=jnp.float32)
        for h in range(2):
            at = slice(h * LANES, (h + 1) * LANES)
            we_ref[b, :, at] = jnp.exp(dots[:, at] * tscale_ref[...])
        wsx_ref[b] = jnp.exp(logits * (1.0 / STUDENT_TEMP))

    def own_tiles(begin, end, stage):
        arrived(stage, amounts[stage])
        arrived(stage + 1, amounts[stage + 1])

        def pair(b, carry):
            own_tile(b)
            own_tile(HALF + b)
            return carry

        lax.fori_loop(begin, end, pair, 0)

    def scale_own():
        ucol_ref[...] = jnp.concatenate(
            [jnp.transpose(jnp.broadcast_to(u_ref[2 * z + h], (LANES, LANES))) for h in range(2)], axis=0
        )

        def scaled(b, carry):
            for h in range(2):
                at = slice(h * LANES, (h + 1) * LANES)
                we_ref[b, :, at] = we_ref[b, :, at] * ucol_ref[...]
            return carry

        lax.fori_loop(0, NZ, scaled, 0, unroll=2)

    gather_z()

    for it in range(ITERS):
        if it > 0:
            def proto_tiles(g, carry):
                totals = [None] * 4
                for r in range(0, B, 8):
                    c = crep_ref[r:r + 8]
                    for i in range(4):
                        term = e_ref[4 * g + i, r:r + 8] * c
                        totals[i] = term if r == 0 else totals[i] + term
                for i in range(4):
                    pr_ref[4 * g + i] = jnp.sum(totals[i], axis=0, keepdims=True)
                return carry

            lax.fori_loop(0, TILES // 4, proto_tiles, 0, unroll=2)
            send_protos(it)
        if it == 1:
            gather_one()
            own = columns(z)
            raw = jnp.transpose(tw_ref[:, own].astype(jnp.float32))
            twt_ref[...] = raw.astype(jnp.bfloat16)
            pltpu.make_async_copy(sbuf_ref, sbuf_ref, srecv_sem).wait()
            student = ssend_ref[...]
            for k in range(NJ - 1):
                student = student + sbuf_ref[k]
            inverse = float(PROTOS) / student
            xsend_ref[:, B:] = inverse
            srep_ref[...] = jnp.transpose(jnp.broadcast_to(inverse, (LANES, B)))
            scale = lax.rsqrt(jnp.sum(raw * raw, axis=1, keepdims=True) + EPSILON) * (1.0 / TEACHER_TEMP)
            tscale_ref[...] = jnp.broadcast_to(scale, (WIDE, LANES))
            swt_ref[...] = jnp.transpose(ws_ref[:, own].astype(jnp.float32)).astype(jnp.bfloat16)
            arrived(1, amounts[1])
            arrived(2, amounts[2])
            gather_two(0, EARLY, 3)
        if it == 2:
            arrived(3, amounts[3])
            arrived(4, amounts[4])
            gather_two(EARLY, HALF, 5)
            gather_core(0, EARLY, 7)
            own_tiles(0, EARLY, 7)
        last = it == ITERS - 1

        def crop_tile(t, acc):
            scaled = e_ref[t] * u_ref[t]
            if last:
                e_ref[t] = scaled
            return acc + scaled

        acc = jnp.zeros((B, LANES), jnp.float32)
        for part in range(2):
            receive_protos(it, part)
            acc = lax.fori_loop(part * HTILES, (part + 1) * HTILES, crop_tile, acc, unroll=4)
        row = jnp.sum(jnp.transpose(acc), axis=0, keepdims=True)
        csend_ref[it] = row
        for k in range(1, NJ):
            pltpu.make_async_remote_copy(
                src_ref=csend_ref.at[it],
                dst_ref=cbuf_ref.at[it, k - 1],
                send_sem=csend_sem.at[it],
                recv_sem=crecv_sem.at[it],
                device_id=jpeer(k),
                device_id_type=MESH,
            ).start()
        if last:
            arrived(5, amounts[5])
            arrived(6, amounts[6])
            gather_core(EARLY, HALF, 9)
        got = cbuf_ref.at[it]
        pltpu.make_async_copy(got, got, crecv_sem.at[it]).wait()
        for k in range(NJ - 1):
            row = row + cbuf_ref[it, k]
        crop_scale = 1.0 / row
        if last:
            crop_scale = crop_scale * float(PROTOS)
            xsend_ref[:, :B] = crop_scale
            for k in Z_ORDER:
                pltpu.make_async_remote_copy(
                    src_ref=xsend_ref,
                    dst_ref=xbuf_ref.at[k - 1],
                    send_sem=xsend_sem,
                    recv_sem=xrecv_sem.at[k - 1],
                    device_id=zpeer(k),
                    device_id_type=MESH,
                ).start()
        crep_ref[...] = jnp.transpose(jnp.broadcast_to(crop_scale, (LANES, B)))

    weight_factor = math.sqrt(D / CROPS)
    feature_factor = math.sqrt(D / PROTOS)

    def grad_tile(t, carry):
        c = crep_ref[...]
        halves = [s_ref[2 * t + h] * srep_ref[...] - e_ref[2 * t + h] * c for h in range(2)]
        grad = jnp.concatenate([half.astype(jnp.bfloat16) for half in halves], axis=1)
        grad_ref[:, columns(t)] = grad
        return carry

    lax.fori_loop(0, WTILES, grad_tile, 0, unroll=4)

    feature = lax.dot_general(
        grad_ref[...], ws_ref[...], (((1,), (1,)), ((), ())), preferred_element_type=jnp.float32
    ) * feature_factor
    for i in range(NJ):
        rows = feature[i * FROWS:(i + 1) * FROWS]
        fsend_ref[i] = jnp.concatenate([rows[:, :LANES], rows[:, LANES:]], axis=0).astype(jnp.bfloat16)
    for k in range(1, NJ):
        pltpu.make_async_remote_copy(
            src_ref=fsend_ref.at[lax.rem(j + k, NJ)],
            dst_ref=fbuf_ref.at[k - 1],
            send_sem=fsend_sem,
            recv_sem=frecv_sem,
            device_id=jpeer(k),
            device_id_type=MESH,
        ).start()

    own_tiles(EARLY, HALF, 9)
    scale_own()
    def block(b, scales):
        grad = (wsx_ref[b] * scales[:, B:] - we_ref[b] * scales[:, :B]).astype(jnp.bfloat16)
        return lax.dot_general(
            all_ref[1, b].reshape(D, B), grad, (((1,), (1,)), ((), ())), preferred_element_type=jnp.float32
        )

    near = Z_ORDER[::-1]
    for group in (near[:4], near[4:8], near[8:12], near[12:14], near[14:]):
        for k in group:
            slot = xbuf_ref.at[k - 1]
            pltpu.make_async_copy(slot, slot, xrecv_sem.at[k - 1]).wait()
        total = block(z, xsend_ref[...]) if group[0] == near[0] else wacc_ref[...]
        for k in group:
            total = total + block(lax.rem(z + NZ - k, NZ), xbuf_ref[k - 1])
        wacc_ref[...] = total
    weight = (wacc_ref[...] * weight_factor).astype(jnp.bfloat16)
    for b in range(NZ):
        wsend_ref[b] = weight[b * ROWS:(b + 1) * ROWS]
    for k in Z_ORDER:
        pltpu.make_async_remote_copy(
            src_ref=wsend_ref.at[lax.rem(z + k, NZ)],
            dst_ref=wrecv_ref.at[k - 1],
            send_sem=wsend_sem,
            recv_sem=wrecv_sem,
            device_id=zpeer(k),
            device_id_type=MESH,
        ).start()

    whole = fbuf_ref
    pltpu.make_async_copy(whole, whole, frecv_sem).wait()
    total = fsend_ref[j].astype(jnp.float32)
    for k in range(NJ - 1):
        total = total + fbuf_ref[k].astype(jnp.float32)
    unit_grad = jnp.concatenate([total[:FROWS], total[FROWS:]], axis=1)
    mine = pl.ds(pl.multiple_of(j * FROWS, FROWS), FROWS)
    unit = zfull_ref[mine, :]
    along = jnp.sum(unit * unit_grad, axis=1, keepdims=True)
    length = zlen_ref[mine, :]
    rows = unit_grad - unit * along
    gsend_ref[...] = jnp.concatenate([rows[:, :LANES] / length, rows[:, LANES:] / length], axis=0).astype(jnp.bfloat16)
    for k in range(1, NJ):
        pltpu.make_async_remote_copy(
            src_ref=gsend_ref,
            dst_ref=gbuf_ref.at[j],
            send_sem=gsend_sem,
            recv_sem=grecv_sem,
            device_id=jpeer(k),
            device_id_type=MESH,
        ).start()
    gbuf_ref[j] = gsend_ref[...]

    got = gbuf_ref.at[pl.ds(0, NJ - 1)]
    pltpu.make_async_copy(got, got, grecv_sem).wait()
    for i in range(NJ // 2):
        one = gbuf_ref[2 * i].astype(jnp.float32)
        two = gbuf_ref[2 * i + 1].astype(jnp.float32)
        left = jnp.concatenate([one[:FROWS], two[:FROWS]], axis=0)
        right = jnp.concatenate([one[FROWS:], two[FROWS:]], axis=0)
        fout_ref[2 * FROWS * i:2 * FROWS * (i + 1), :] = jnp.concatenate([left, right], axis=1).astype(jnp.bfloat16)

    for it in range(ITERS):
        for part in range(2):
            whole = pbuf_ref.at[it, part]
            pltpu.make_async_copy(whole, whole, psend_sem.at[it, part]).wait()
        got = cbuf_ref.at[it]
        pltpu.make_async_copy(got, got, csend_sem.at[it]).wait()
    pltpu.make_async_copy(sbuf_ref, sbuf_ref, ssend_sem).wait()
    pltpu.make_async_copy(fbuf_ref, fbuf_ref, fsend_sem).wait()
    pltpu.make_async_copy(fbuf_ref, fbuf_ref, gsend_sem).wait()
    pltpu.make_async_copy(xbuf_ref, xbuf_ref, xsend_sem).wait()
    for stage in range(len(amounts)):
        pltpu.make_async_copy(amounts[stage], amounts[stage], gather_send.at[stage]).wait()

    pltpu.make_async_copy(wrecv_ref, wrecv_ref, wrecv_sem).wait()
    wout_ref[:, columns(z)] = wsend_ref[z]
    for k in range(1, NZ):
        wout_ref[:, columns(lax.rem(z + NZ - k, NZ))] = wrecv_ref[k - 1]
    pltpu.make_async_copy(wrecv_ref, wrecv_ref, wsend_sem).wait()


def shards(teacher_feats, student_feats, teacher_weight, student_weight):
    f32, bf16 = jnp.float32, jnp.bfloat16
    vmem, dma = pltpu.VMEM, pltpu.SemaphoreType.DMA
    scratch = [
        vmem((B, D), bf16),
        vmem((B, D), bf16),
        vmem((D, C), bf16),
        vmem((D, C), bf16),
        vmem((TILES, B, LANES), f32),
        vmem((TILES, B, LANES), f32),
        vmem((D, C), bf16),
        vmem((B, C), bf16),
        vmem((2, NZ, NY, NX, ROWS, D), bf16),
        vmem((NZ, WIDE, B), f32),
        vmem((NZ, WIDE, B), f32),
        vmem((B, D), bf16),
        vmem((B, D), bf16),
        vmem((D, B), f32),
        vmem((D, B), f32),
        vmem((B, D), f32),
        vmem((B, LANES), f32),
        vmem((WIDE, D), bf16),
        vmem((WIDE, D), bf16),
        vmem((WIDE, LANES), f32),
        vmem((WIDE, LANES), f32),
        vmem((D, WIDE), f32),
        vmem((NZ, ROWS, WIDE), bf16),
        vmem((NZ - 1, ROWS, WIDE), bf16),
        vmem((1, 2 * B), f32),
        vmem((NZ - 1, 1, 2 * B), f32),
        vmem((TILES, 1, LANES), f32),
        vmem((2, HTILES, LANES), f32),
        vmem((ITERS, 2, HTILES, LANES), bf16),
        vmem((ITERS, 2, NZ - 1, HTILES, LANES), bf16),
        vmem((TILES, 1, LANES), f32),
        vmem((B, LANES), f32),
        vmem((B, LANES), f32),
        vmem((ITERS, 1, B), f32),
        vmem((ITERS, NJ - 1, 1, B), f32),
        vmem((1, B), f32),
        vmem((NJ - 1, 1, B), f32),
        vmem((NJ, 2 * FROWS, LANES), bf16),
        vmem((NJ - 1, 2 * FROWS, LANES), bf16),
        vmem((2 * FROWS, LANES), bf16),
        vmem((NJ, 2 * FROWS, LANES), bf16),
        dma((ITERS, 2)), dma((ITERS, 2)), dma((ITERS,)), dma((ITERS,)), dma, dma,
        dma, dma, dma, dma, dma((3,)), dma((PARTS,)),
        dma((11,)), dma((11,)), dma, dma((NZ - 1,)), dma, dma,
    ]
    return pl.pallas_call(
        kernel,
        out_shape=(jax.ShapeDtypeStruct((ROWS, C), bf16), jax.ShapeDtypeStruct((B, D), bf16)),
        in_specs=[pl.BlockSpec(memory_space=pltpu.HBM)] * 4,
        out_specs=(pl.BlockSpec(memory_space=pltpu.VMEM), pl.BlockSpec(memory_space=pltpu.VMEM)),
        scratch_shapes=scratch,
        compiler_params=pltpu.CompilerParams(
            collective_id=0, has_side_effects=True, vmem_limit_bytes=(536 << 20) // 10
        ),
        cost_estimate=pl.CostEstimate(
            flops=8 * B * C * D, bytes_accessed=4 * D * C + 6 * B * D, transcendentals=2 * B * C
        ),
    )(teacher_feats, student_feats, teacher_weight, student_weight)


def solution(mesh):
    return jax.shard_map(
        shards,
        mesh=mesh,
        in_specs=(P("batch", None), P("batch", None), P(None, "proto"), P(None, "proto")),
        out_specs=(P("batch", "proto"), P("batch", None)),
        check_vma=False,
    )
```

```python
import functools
import math

import jax
import jax.numpy as jnp
from jax import lax
from jax.experimental import pallas as pl
from jax.experimental.pallas import tpu as pltpu
from jax.sharding import PartitionSpec as P

ITERS = 3
TEACHER_TEMP = 0.07
STUDENT_TEMP = 0.1
EPSILON = 1e-06
MESH = pl.DeviceIdType.MESH

NZ = 16
NJ = 32
D = 256
B = 256
C = 4096
PROTOS = C * NJ
CROPS = B * NZ
LANES = 128
TILES = C // LANES
HTILES = TILES // 2
WIDE = 256
WTILES = C // WIDE
PARTS = 4
PART = C // PARTS
ROWS = D // NZ
NX, NY = 4, 4
HALF = NZ // 2
EARLY = 3
FROWS = B // NJ
Z_ORDER = sorted(range(1, NZ), key=lambda k: -min(k, NZ - k))
PLANE = sorted(
    ((dy, dx, dc) for dy in range(NY) for dx in range(NX) for dc in range(2) if dy or dx or dc),
    key=lambda t: -(min(t[0], NY - t[0]) + min(t[1], NX - t[1])),
)


def kernel(
    tf_hbm, sf_hbm, tw_hbm, sw_hbm, wout_ref, fout_ref,
    tf_ref, sf_ref, tw_ref, sw_ref,
    e_ref, s_ref, ws_ref, grad_ref, all_ref, we_ref, wsx_ref,
    zt_ref, zs_ref, ztt_ref, zst_ref, zfull_ref, zlen_ref,
    twt_ref, swt_ref, tscale_ref, ucol_ref, wacc_ref, wsend_ref, wrecv_ref, xsend_ref, xbuf_ref,
    pr_ref, pf_ref, psend_ref, pbuf_ref, u_ref, crep_ref, srep_ref,
    csend_ref, cbuf_ref, ssend_ref, sbuf_ref,
    fsend_ref, fbuf_ref, gsend_ref, gbuf_ref,
    psend_sem, precv_sem, csend_sem, crecv_sem, ssend_sem, srecv_sem,
    fsend_sem, frecv_sem, gsend_sem, grecv_sem, load_sem, tload_sem,
    gather_send, gather_recv, xsend_sem, xrecv_sem, wsend_sem, wrecv_sem,
):
    z = lax.axis_index("batch")
    j = lax.axis_index("proto")

    def zpeer(k):
        return (lax.rem(z + k, NZ), j)

    core = lax.rem(j, 2)
    x = lax.rem(j // 2, NX)
    y = j // (2 * NX)

    def jindex(k):
        dy, dx, dc = PLANE[k - 1]
        return (lax.rem(y + dy, NY) * NX + lax.rem(x + dx, NX)) * 2 + lax.rem(core + dc, 2)

    def jpeer(k):
        return (z, jindex(k))

    def xpeer(k):
        return (z, (y * NX + lax.rem(x + k, NX)) * 2 + core)

    def ypeer(k):
        return (z, (lax.rem(y + k, NY) * NX + x) * 2 + core)

    barrier = pltpu.get_barrier_semaphore()
    for k in Z_ORDER:
        pl.semaphore_signal(barrier, 1, device_id=zpeer(k), device_id_type=MESH)
    for k in range(1, NJ):
        pl.semaphore_signal(barrier, 1, device_id=jpeer(k), device_id_type=MESH)

    load_tf = pltpu.make_async_copy(tf_hbm, tf_ref, load_sem.at[0])
    load_sf = pltpu.make_async_copy(sf_hbm, sf_ref, load_sem.at[1])
    load_sw = pltpu.make_async_copy(sw_hbm, sw_ref, load_sem.at[2])

    def load_tw(part):
        at = pl.ds(pl.multiple_of(part * PART, PART), PART)
        return pltpu.make_async_copy(tw_hbm.at[:, at], tw_ref.at[:, at], tload_sem.at[part])

    load_tf.start()
    for part in range(PARTS):
        load_tw(part).start()
    load_sf.start()
    load_sw.start()
    load_tf.wait()

    tf = tf_ref[...].astype(jnp.float32)
    zt_ref[...] = (tf * lax.rsqrt(jnp.sum(tf * tf, axis=1, keepdims=True) + EPSILON)).astype(jnp.bfloat16)

    def columns(t):
        return pl.ds(pl.multiple_of(t * WIDE, WIDE), WIDE)

    def inverse_lengths(values):
        return lax.rsqrt(jnp.sum(values * values, axis=0, keepdims=True) + EPSILON)

    def teacher_tile(t, carry):
        raw = tw_ref[:, columns(t)]
        scale = inverse_lengths(raw.astype(jnp.float32)) * (1.0 / TEACHER_TEMP)
        dots = jnp.dot(zt_ref[...], raw, preferred_element_type=jnp.float32)
        e = jnp.exp(dots * scale)
        e_ref[2 * t] = e[:, :LANES]
        e_ref[2 * t + 1] = e[:, LANES:]
        sums = jnp.sum(e, axis=0, keepdims=True)
        pr_ref[2 * t] = sums[:, :LANES]
        pr_ref[2 * t + 1] = sums[:, LANES:]
        return carry

    for part in range(PARTS):
        load_tw(part).wait()
        lax.fori_loop(part * (WTILES // PARTS), (part + 1) * (WTILES // PARTS), teacher_tile, 0, unroll=True)

    def send_protos(it):
        for part in range(2):
            sums = jnp.concatenate([pr_ref[part * HTILES + t] for t in range(HTILES)], axis=0)
            pf_ref[part] = sums
            psend_ref[it, part] = sums.astype(jnp.bfloat16)
        for k in Z_ORDER:
            for part in range(2):
                pltpu.make_async_remote_copy(
                    src_ref=psend_ref.at[it, part],
                    dst_ref=pbuf_ref.at[it, part, k - 1],
                    send_sem=psend_sem.at[it, part],
                    recv_sem=precv_sem.at[it, part],
                    device_id=zpeer(k),
                    device_id_type=MESH,
                ).start()

    def receive_protos(it, part):
        whole = pbuf_ref.at[it, part]
        pltpu.make_async_copy(whole, whole, precv_sem.at[it, part]).wait()
        total = pf_ref[part]
        for k in range(NZ - 1):
            total = total + pbuf_ref[it, part, k].astype(jnp.float32)
        scale = 1.0 / total
        for t in range(HTILES):
            u_ref[part * HTILES + t] = scale[t:t + 1]

    pl.semaphore_wait(barrier, NJ + NZ - 2)
    send_protos(0)

    load_sf.wait()
    load_sw.wait()
    sf = sf_ref[...].astype(jnp.float32)
    slen = jnp.sqrt(jnp.sum(sf * sf, axis=1, keepdims=True) + EPSILON)
    sfull = sf / slen
    zfull_ref[...] = sfull
    zlen_ref[...] = jnp.broadcast_to(slen, (B, LANES))
    zs_ref[...] = sfull.astype(jnp.bfloat16)

    def student_tile(t, acc):
        values = sw_ref[:, columns(t)].astype(jnp.float32)
        ws = (values * inverse_lengths(values)).astype(jnp.bfloat16)
        ws_ref[:, columns(t)] = ws
        dots = jnp.dot(zs_ref[...], ws, preferred_element_type=jnp.float32)
        s = jnp.exp(dots * (1.0 / STUDENT_TEMP))
        s_ref[2 * t] = s[:, :LANES]
        s_ref[2 * t + 1] = s[:, LANES:]
        return acc + s[:, :LANES] + s[:, LANES:]

    sacc = lax.fori_loop(0, WTILES, student_tile, jnp.zeros((B, LANES), jnp.float32), unroll=2)
    ssend_ref[...] = jnp.sum(jnp.transpose(sacc), axis=0, keepdims=True)
    for k in range(1, NJ):
        pltpu.make_async_remote_copy(
            src_ref=ssend_ref,
            dst_ref=sbuf_ref.at[k - 1],
            send_sem=ssend_sem,
            recv_sem=srecv_sem,
            device_id=jpeer(k),
            device_id_type=MESH,
        ).start()

    def post(src, dst, stage, peer):
        pltpu.make_async_remote_copy(
            src_ref=src,
            dst_ref=dst,
            send_sem=gather_send.at[stage],
            recv_sem=gather_recv.at[stage],
            device_id=peer,
            device_id_type=MESH,
        ).start()

    def arrived(stage, amount):
        pltpu.make_async_copy(amount, amount, gather_recv.at[stage]).wait()

    amounts = (
        all_ref.at[0, pl.ds(0, NZ - 1), 0, 0],
        all_ref.at[0, pl.ds(0, HALF), 0, pl.ds(0, NX - 1)],
        all_ref.at[0, pl.ds(0, HALF), 0, pl.ds(0, NX - 1)],
        all_ref.at[0, pl.ds(0, EARLY), pl.ds(0, NY - 1)],
        all_ref.at[0, pl.ds(0, EARLY), pl.ds(0, NY - 1)],
        all_ref.at[0, pl.ds(0, HALF - EARLY), pl.ds(0, NY - 1)],
        all_ref.at[0, pl.ds(0, HALF - EARLY), pl.ds(0, NY - 1)],
        all_ref.at[0, pl.ds(0, EARLY)],
        all_ref.at[0, pl.ds(0, EARLY)],
        all_ref.at[0, pl.ds(0, HALF - EARLY)],
        all_ref.at[0, pl.ds(0, HALF - EARLY)],
    )
    first, second = pl.ds(0, HALF), pl.ds(HALF, HALF)

    def gather_z():
        rows = pl.ds(pl.multiple_of((j // 2) * ROWS, ROWS), ROWS)
        ztt_ref[...] = jnp.transpose(zt_ref[...].astype(jnp.float32))
        zst_ref[...] = jnp.transpose(zs_ref[...].astype(jnp.float32))
        all_ref[core, z, y, x] = jnp.where(core == 0, ztt_ref[rows, :], zst_ref[rows, :]).astype(jnp.bfloat16)
        mine = all_ref.at[core, z, y, x]
        for k in Z_ORDER:
            post(mine, mine, 0, zpeer(k))

    def gather_one():
        arrived(0, amounts[0])
        for k in (2, 1, 3):
            one = all_ref.at[core, first, y, x]
            post(one, one, 1, xpeer(k))
            two = all_ref.at[core, second, y, x]
            post(two, two, 2, ypeer(k))

    def gather_two(begin, end, stage):
        for k in (2, 1, 3):
            one = all_ref.at[core, pl.ds(begin, end - begin), y]
            post(one, one, stage, ypeer(k))
            two = all_ref.at[core, pl.ds(HALF + begin, end - begin), :, x]
            post(two, two, stage + 1, xpeer(k))

    def gather_core(begin, end, stage):
        for half in range(2):
            mine = all_ref.at[core, pl.ds(half * HALF + begin, end - begin)]
            post(mine, mine, stage + half, (z, j + 1 - 2 * core))

    def own_tile(b):
        dots = jnp.dot(twt_ref[...], all_ref[0, b].reshape(D, B), preferred_element_type=jnp.float32)
        logits = jnp.dot(swt_ref[...], all_ref[1, b].reshape(D, B), preferred_element_type=jnp.float32)
        for h in range(2):
            at = slice(h * LANES, (h + 1) * LANES)
            we_ref[b, :, at] = jnp.exp(dots[:, at] * tscale_ref[...])
        wsx_ref[b] = jnp.exp(logits * (1.0 / STUDENT_TEMP))

    def own_tiles(begin, end, stage):
        arrived(stage, amounts[stage])
        arrived(stage + 1, amounts[stage + 1])

        def pair(b, carry):
            own_tile(b)
            own_tile(HALF + b)
            return carry

        lax.fori_loop(begin, end, pair, 0)

    def scale_own():
        ucol_ref[...] = jnp.concatenate(
            [jnp.transpose(jnp.broadcast_to(u_ref[2 * z + h], (LANES, LANES))) for h in range(2)], axis=0
        )

        def scaled(b, carry):
            for h in range(2):
                at = slice(h * LANES, (h + 1) * LANES)
                we_ref[b, :, at] = we_ref[b, :, at] * ucol_ref[...]
            return carry

        lax.fori_loop(0, NZ, scaled, 0, unroll=2)

    gather_z()

    for it in range(ITERS):
        if it > 0:
            def proto_tiles(g, carry):
                totals = [None] * 4
                for r in range(0, B, 8):
                    c = crep_ref[r:r + 8]
                    for i in range(4):
                        term = e_ref[4 * g + i, r:r + 8] * c
                        totals[i] = term if r == 0 else totals[i] + term
                for i in range(4):
                    pr_ref[4 * g + i] = jnp.sum(totals[i], axis=0, keepdims=True)
                return carry

            lax.fori_loop(0, TILES // 4, proto_tiles, 0, unroll=2)
            send_protos(it)
        if it == 1:
            gather_one()
            own = columns(z)
            raw = jnp.transpose(tw_ref[:, own].astype(jnp.float32))
            twt_ref[...] = raw.astype(jnp.bfloat16)
            pltpu.make_async_copy(sbuf_ref, sbuf_ref, srecv_sem).wait()
            student = ssend_ref[...]
            for k in range(NJ - 1):
                student = student + sbuf_ref[k]
            inverse = float(PROTOS) / student
            xsend_ref[:, B:] = inverse
            srep_ref[...] = jnp.transpose(jnp.broadcast_to(inverse, (LANES, B)))
            scale = lax.rsqrt(jnp.sum(raw * raw, axis=1, keepdims=True) + EPSILON) * (1.0 / TEACHER_TEMP)
            tscale_ref[...] = jnp.broadcast_to(scale, (WIDE, LANES))
            swt_ref[...] = jnp.transpose(ws_ref[:, own].astype(jnp.float32)).astype(jnp.bfloat16)
            arrived(1, amounts[1])
            arrived(2, amounts[2])
            gather_two(0, EARLY, 3)
        if it == 2:
            arrived(3, amounts[3])
            arrived(4, amounts[4])
            gather_two(EARLY, HALF, 5)
            gather_core(0, EARLY, 7)
            own_tiles(0, EARLY, 7)
        last = it == ITERS - 1

        def crop_tile(t, acc):
            scaled = e_ref[t] * u_ref[t]
            if last:
                e_ref[t] = scaled
            return acc + scaled

        acc = jnp.zeros((B, LANES), jnp.float32)
        for part in range(2):
            receive_protos(it, part)
            acc = lax.fori_loop(part * HTILES, (part + 1) * HTILES, crop_tile, acc, unroll=4)
        row = jnp.sum(jnp.transpose(acc), axis=0, keepdims=True)
        csend_ref[it] = row
        for k in range(1, NJ):
            pltpu.make_async_remote_copy(
                src_ref=csend_ref.at[it],
                dst_ref=cbuf_ref.at[it, k - 1],
                send_sem=csend_sem.at[it],
                recv_sem=crecv_sem.at[it],
                device_id=jpeer(k),
                device_id_type=MESH,
            ).start()
        if last:
            arrived(5, amounts[5])
            arrived(6, amounts[6])
            gather_core(EARLY, HALF, 9)
        got = cbuf_ref.at[it]
        pltpu.make_async_copy(got, got, crecv_sem.at[it]).wait()
        for k in range(NJ - 1):
            row = row + cbuf_ref[it, k]
        crop_scale = 1.0 / row
        if last:
            crop_scale = crop_scale * float(PROTOS)
            xsend_ref[:, :B] = crop_scale
            for k in Z_ORDER:
                pltpu.make_async_remote_copy(
                    src_ref=xsend_ref,
                    dst_ref=xbuf_ref.at[k - 1],
                    send_sem=xsend_sem,
                    recv_sem=xrecv_sem.at[k - 1],
                    device_id=zpeer(k),
                    device_id_type=MESH,
                ).start()
        crep_ref[...] = jnp.transpose(jnp.broadcast_to(crop_scale, (LANES, B)))

    weight_factor = math.sqrt(D / CROPS)
    feature_factor = math.sqrt(D / PROTOS)

    def grad_tile(t, carry):
        c = crep_ref[...]
        halves = [s_ref[2 * t + h] * srep_ref[...] - e_ref[2 * t + h] * c for h in range(2)]
        grad = jnp.concatenate([half.astype(jnp.bfloat16) for half in halves], axis=1)
        grad_ref[:, columns(t)] = grad
        return carry

    lax.fori_loop(0, WTILES, grad_tile, 0, unroll=4)

    feature = lax.dot_general(
        grad_ref[...], ws_ref[...], (((1,), (1,)), ((), ())), preferred_element_type=jnp.float32
    ) * feature_factor
    for i in range(NJ):
        rows = feature[i * FROWS:(i + 1) * FROWS]
        fsend_ref[i] = jnp.concatenate([rows[:, :LANES], rows[:, LANES:]], axis=0).astype(jnp.bfloat16)
    for k in range(1, NJ):
        pltpu.make_async_remote_copy(
            src_ref=fsend_ref.at[jindex(k)],
            dst_ref=fbuf_ref.at[k - 1],
            send_sem=fsend_sem,
            recv_sem=frecv_sem,
            device_id=jpeer(k),
            device_id_type=MESH,
        ).start()

    own_tiles(EARLY, HALF, 9)
    scale_own()
    def block(b, scales):
        grad = (wsx_ref[b] * scales[:, B:] - we_ref[b] * scales[:, :B]).astype(jnp.bfloat16)
        return lax.dot_general(
            all_ref[1, b].reshape(D, B), grad, (((1,), (1,)), ((), ())), preferred_element_type=jnp.float32
        )

    near = Z_ORDER[::-1]
    for group in (near[:4], near[4:8], near[8:12], near[12:14], near[14:]):
        for k in group:
            slot = xbuf_ref.at[k - 1]
            pltpu.make_async_copy(slot, slot, xrecv_sem.at[k - 1]).wait()
        total = block(z, xsend_ref[...]) if group[0] == near[0] else wacc_ref[...]
        for k in group:
            total = total + block(lax.rem(z + NZ - k, NZ), xbuf_ref[k - 1])
        wacc_ref[...] = total
    weight = (wacc_ref[...] * weight_factor).astype(jnp.bfloat16)
    for b in range(NZ):
        wsend_ref[b] = weight[b * ROWS:(b + 1) * ROWS]
    for k in Z_ORDER:
        pltpu.make_async_remote_copy(
            src_ref=wsend_ref.at[lax.rem(z + k, NZ)],
            dst_ref=wrecv_ref.at[k - 1],
            send_sem=wsend_sem,
            recv_sem=wrecv_sem,
            device_id=zpeer(k),
            device_id_type=MESH,
        ).start()

    whole = fbuf_ref
    pltpu.make_async_copy(whole, whole, frecv_sem).wait()
    total = fsend_ref[j].astype(jnp.float32)
    for k in range(NJ - 1):
        total = total + fbuf_ref[k].astype(jnp.float32)
    unit_grad = jnp.concatenate([total[:FROWS], total[FROWS:]], axis=1)
    mine = pl.ds(pl.multiple_of(j * FROWS, FROWS), FROWS)
    unit = zfull_ref[mine, :]
    along = jnp.sum(unit * unit_grad, axis=1, keepdims=True)
    length = zlen_ref[mine, :]
    rows = unit_grad - unit * along
    gsend_ref[...] = jnp.concatenate([rows[:, :LANES] / length, rows[:, LANES:] / length], axis=0).astype(jnp.bfloat16)
    for k in range(1, NJ):
        pltpu.make_async_remote_copy(
            src_ref=gsend_ref,
            dst_ref=gbuf_ref.at[j],
            send_sem=gsend_sem,
            recv_sem=grecv_sem,
            device_id=jpeer(k),
            device_id_type=MESH,
        ).start()
    gbuf_ref[j] = gsend_ref[...]

    got = gbuf_ref.at[pl.ds(0, NJ - 1)]
    pltpu.make_async_copy(got, got, grecv_sem).wait()
    for i in range(NJ // 2):
        one = gbuf_ref[2 * i].astype(jnp.float32)
        two = gbuf_ref[2 * i + 1].astype(jnp.float32)
        left = jnp.concatenate([one[:FROWS], two[:FROWS]], axis=0)
        right = jnp.concatenate([one[FROWS:], two[FROWS:]], axis=0)
        fout_ref[2 * FROWS * i:2 * FROWS * (i + 1), :] = jnp.concatenate([left, right], axis=1).astype(jnp.bfloat16)

    for it in range(ITERS):
        for part in range(2):
            whole = pbuf_ref.at[it, part]
            pltpu.make_async_copy(whole, whole, psend_sem.at[it, part]).wait()
        got = cbuf_ref.at[it]
        pltpu.make_async_copy(got, got, csend_sem.at[it]).wait()
    pltpu.make_async_copy(sbuf_ref, sbuf_ref, ssend_sem).wait()
    pltpu.make_async_copy(fbuf_ref, fbuf_ref, fsend_sem).wait()
    pltpu.make_async_copy(fbuf_ref, fbuf_ref, gsend_sem).wait()
    pltpu.make_async_copy(xbuf_ref, xbuf_ref, xsend_sem).wait()
    for stage in range(len(amounts)):
        pltpu.make_async_copy(amounts[stage], amounts[stage], gather_send.at[stage]).wait()

    pltpu.make_async_copy(wrecv_ref, wrecv_ref, wrecv_sem).wait()
    wout_ref[:, columns(z)] = wsend_ref[z]
    for k in range(1, NZ):
        wout_ref[:, columns(lax.rem(z + NZ - k, NZ))] = wrecv_ref[k - 1]
    pltpu.make_async_copy(wrecv_ref, wrecv_ref, wsend_sem).wait()


def shards(teacher_feats, student_feats, teacher_weight, student_weight):
    f32, bf16 = jnp.float32, jnp.bfloat16
    vmem, dma = pltpu.VMEM, pltpu.SemaphoreType.DMA
    scratch = [
        vmem((B, D), bf16),
        vmem((B, D), bf16),
        vmem((D, C), bf16),
        vmem((D, C), bf16),
        vmem((TILES, B, LANES), f32),
        vmem((TILES, B, LANES), f32),
        vmem((D, C), bf16),
        vmem((B, C), bf16),
        vmem((2, NZ, NY, NX, ROWS, D), bf16),
        vmem((NZ, WIDE, B), f32),
        vmem((NZ, WIDE, B), f32),
        vmem((B, D), bf16),
        vmem((B, D), bf16),
        vmem((D, B), f32),
        vmem((D, B), f32),
        vmem((B, D), f32),
        vmem((B, LANES), f32),
        vmem((WIDE, D), bf16),
        vmem((WIDE, D), bf16),
        vmem((WIDE, LANES), f32),
        vmem((WIDE, LANES), f32),
        vmem((D, WIDE), f32),
        vmem((NZ, ROWS, WIDE), bf16),
        vmem((NZ - 1, ROWS, WIDE), bf16),
        vmem((1, 2 * B), f32),
        vmem((NZ - 1, 1, 2 * B), f32),
        vmem((TILES, 1, LANES), f32),
        vmem((2, HTILES, LANES), f32),
        vmem((ITERS, 2, HTILES, LANES), bf16),
        vmem((ITERS, 2, NZ - 1, HTILES, LANES), bf16),
        vmem((TILES, 1, LANES), f32),
        vmem((B, LANES), f32),
        vmem((B, LANES), f32),
        vmem((ITERS, 1, B), f32),
        vmem((ITERS, NJ - 1, 1, B), f32),
        vmem((1, B), f32),
        vmem((NJ - 1, 1, B), f32),
        vmem((NJ, 2 * FROWS, LANES), bf16),
        vmem((NJ - 1, 2 * FROWS, LANES), bf16),
        vmem((2 * FROWS, LANES), bf16),
        vmem((NJ, 2 * FROWS, LANES), bf16),
        dma((ITERS, 2)), dma((ITERS, 2)), dma((ITERS,)), dma((ITERS,)), dma, dma,
        dma, dma, dma, dma, dma((3,)), dma((PARTS,)),
        dma((11,)), dma((11,)), dma, dma((NZ - 1,)), dma, dma,
    ]
    return pl.pallas_call(
        kernel,
        out_shape=(jax.ShapeDtypeStruct((ROWS, C), bf16), jax.ShapeDtypeStruct((B, D), bf16)),
        in_specs=[pl.BlockSpec(memory_space=pltpu.HBM)] * 4,
        out_specs=(pl.BlockSpec(memory_space=pltpu.VMEM), pl.BlockSpec(memory_space=pltpu.VMEM)),
        scratch_shapes=scratch,
        compiler_params=pltpu.CompilerParams(
            collective_id=0, has_side_effects=True, vmem_limit_bytes=(536 << 20) // 10
        ),
        cost_estimate=pl.CostEstimate(
            flops=8 * B * C * D, bytes_accessed=4 * D * C + 6 * B * D, transcendentals=2 * B * C
        ),
    )(teacher_feats, student_feats, teacher_weight, student_weight)


def solution(mesh):
    return jax.shard_map(
        shards,
        mesh=mesh,
        in_specs=(P("batch", None), P("batch", None), P(None, "proto"), P(None, "proto")),
        out_specs=(P("batch", "proto"), P("batch", None)),
        check_vma=False,
    )
```
